512 devices in a mesh: dp: 32 (over y, x, core), prompt: 16 (over z).
Axes of the slice: x: 4, y: 4, z: 16, core: 2. Of those that a mesh axis runs over, the one named last changes fastest.
Arguments:
- queries: bfloat16 [16, 32, 256, 4096], P('prompt', 'dp'), may hold values from -27 to 27
- send_list: int32 [16, 32, 256], P('prompt', 'dp'), may hold values from 0 to 255, each once within a row
- recv_list: int32 [16, 32, 256], P('prompt', 'dp'), may hold values from 0 to 255, each once within a row
- slot_pos: int32 [16, 32, 256], P('prompt', 'dp'), may hold values from 0 to 383
- pack_seq: int32 [16, 32, 16], P('prompt', 'dp'), may hold values from 0 to 15, each once within a row
- seq_kv: bfloat16 [32, 16, 384, 1024], P('dp', 'prompt'), may hold values from -6 to 6
Outputs:
- attended: bfloat16 [16, 32, 256, 4096], P('prompt', 'dp')
The draws below stay inside these ranges and needn't reach their ends.
Inputs may be any that keep to these rules, and one draw needn't show every extreme that they name: Each pack device's row of pack_seq names every sequence once.
All inputs are finite; a program needn't handle non-finite values.
Results may differ from the reference program's by a relative error of at most 0.0036.
Values may be sent and summed in bfloat16 or wider, within the bound.
No kernel may reach another device: no remote copies, remote signals or barrier semaphores. Data moves between devices by JAX's collectives and lax.ppermute only.
A program may use at most 128 MiB of HBM per device.

```python
import math
import jax
import jax.numpy as jnp
from jax import lax

HD = 128
QH = 32
KVH = 4
ROW_DEV = 256
SEQ = 384
RPS = 16
N_DP = 32
N_PROMPT = 16


def draw_queries(key, part):
    key = jax.random.fold_in(key, 11)
    extent = (N_PROMPT, N_DP, ROW_DEV, QH * HD)
    values = jnp.clip(jax.random.normal(key, extent, jnp.float32), -6.0, 6.0)
    return values.astype(jnp.bfloat16)


def draw_seq_kv(key, part):
    key = jax.random.fold_in(key, 23)
    extent = (N_DP, N_PROMPT, SEQ, 2 * KVH * HD)
    values = jnp.clip(jax.random.normal(key, extent, jnp.float32), -6.0, 6.0)
    return values.astype(jnp.bfloat16)


def touch_ends(array, own_key, smallest, high):
    spot = [jax.random.randint(jax.random.fold_in(own_key, axis), (), 0, length) for axis, length in enumerate(array.shape)]
    longest = array.shape.index(max(array.shape))
    next_to = spot[:longest] + [(spot[longest] + 1) % array.shape[longest]] + spot[longest + 1:]
    return array.at[tuple(spot)].set(smallest).at[tuple(next_to)].set(high)


def setup_inputs(seed: int = 0) -> dict:
    splits = jax.random.split(jax.random.key(seed), 7)
    return {
        "queries": draw_queries(jax.random.fold_in(splits[6], 71), 0),
        "send_list": jax.vmap(lambda own: jax.random.permutation(own, ROW_DEV))(jax.random.split(splits[1], N_PROMPT * N_DP)).reshape((N_PROMPT, N_DP, ROW_DEV)).astype(jnp.int32),
        "recv_list": jax.vmap(lambda own: jax.random.permutation(own, ROW_DEV))(jax.random.split(splits[2], N_PROMPT * N_DP)).reshape((N_PROMPT, N_DP, ROW_DEV)).astype(jnp.int32),
        "slot_pos": touch_ends(jax.random.randint(splits[3], (N_PROMPT, N_DP, ROW_DEV), 0, SEQ), jax.random.fold_in(splits[3], 1), 0, SEQ - 1).astype(jnp.int32),
        "pack_seq": jax.vmap(lambda own: jax.random.permutation(own, N_PROMPT))(jax.random.split(splits[4], N_PROMPT * N_DP)).reshape((N_PROMPT, N_DP, N_PROMPT)).astype(jnp.int32),
        "seq_kv": draw_seq_kv(jax.random.fold_in(splits[6], 71), 0),
    }


def attend(query_rows, seq_block, positions):
    groups = QH // KVH
    row_count = query_rows.shape[0]
    query_heads = query_rows.astype(jnp.float32).reshape(row_count, KVH, groups, HD)
    key_block = seq_block[:, :KVH * HD].astype(jnp.float32).reshape(-1, KVH, HD)
    value_block = seq_block[:, KVH * HD:].astype(jnp.float32).reshape(-1, KVH, HD)
    scores = jnp.einsum('rkgd,ukd->kgru', query_heads, key_block) / math.sqrt(HD)
    visible = jnp.arange(key_block.shape[0], dtype=jnp.int32)[None, :] <= positions[:, None]
    scores = jnp.where(visible, scores, -jnp.inf)
    row_max = lax.optimization_barrier(jnp.max(scores, axis=-1, keepdims=True))
    exponent = jnp.exp(scores - row_max)
    row_total = lax.optimization_barrier(jnp.sum(exponent, axis=-1))
    weights = exponent.astype(jnp.bfloat16)
    mixed = jnp.einsum('kgru,ukd->rkgd', weights.astype(jnp.float32), value_block)
    mixed = mixed / jnp.transpose(row_total, (2, 0, 1))[..., None]
    return mixed.reshape(row_count, QH * HD)

def scatter_rows(row_block, targets):
    return jnp.zeros_like(row_block).at[targets].set(row_block)

def reference(queries, send_list, recv_list, slot_pos, pack_seq, seq_kv):
    placer = jax.vmap(jax.vmap(scatter_rows))
    ordered = placer(queries, send_list)
    per_peer = ROW_DEV // N_DP
    moved = ordered.reshape(N_PROMPT, N_DP, N_DP, per_peer, QH * HD)
    moved = jnp.transpose(moved, (0, 2, 1, 3, 4)).reshape(queries.shape)
    packed = placer(moved, recv_list)
    flattened = packed.reshape(N_PROMPT * N_DP, ROW_DEV, QH * HD)

    def device_work(inputs):
        query_rows, positions, sequences, device_index = inputs
        column = device_index % N_DP
        grouped = query_rows.reshape(N_PROMPT, RPS, QH * HD)
        grouped_pos = positions.reshape(N_PROMPT, RPS)

        def one_group(group_inputs):
            rows, pos, seq_id = group_inputs
            return attend(rows, seq_kv[column, seq_id], pos).astype(jnp.bfloat16)
        out = lax.map(one_group, (grouped, grouped_pos, sequences))
        return out.reshape(ROW_DEV, QH * HD)
    result = lax.map(device_work, (flattened, slot_pos.reshape(-1, ROW_DEV), pack_seq.reshape(-1, N_PROMPT), jnp.arange(N_PROMPT * N_DP, dtype=jnp.int32)))
    return result.reshape(queries.shape)
```

```python
import functools
import math

import jax
import jax.numpy as jnp
from jax import lax
from jax.experimental import pallas as pl
from jax.experimental.pallas import tpu as pltpu
from jax.sharding import PartitionSpec as P

HD = 128
QH = 32
KVH = 4
GROUPS = QH // KVH
SCALE = math.log2(math.e) / math.sqrt(HD)


def attend_kernel(spots, halves, prev_ref, where_ref, pos_ref, q_ref, *refs):
    del prev_ref
    n = len(spots) * halves
    blocks, out_ref, held, sems = refs[:n], refs[n], refs[n + 1], refs[n + 2]
    copies = []
    for i, spot in enumerate(spots):
        rows = q_ref.shape[0] // len(spots)
        cache_len = blocks[0].shape[0]
        limit = pos_ref[:, spot : spot + 1]
        visible = lax.broadcasted_iota(jnp.int32, (rows, cache_len), 1) <= limit
        for half in range(halves):
            block = blocks[i * halves + half]
            kv_heads = KVH // halves
            for k in range(kv_heads):
                head = half * kv_heads + k
                query = jnp.concatenate(
                    [
                        q_ref[i * rows : (i + 1) * rows, (head * GROUPS + g) * HD : (head * GROUPS + g + 1) * HD]
                        for g in range(GROUPS)
                    ],
                    axis=0,
                )
                scores = lax.dot_general(
                    query,
                    block[:, k * HD : (k + 1) * HD],
                    (((1,), (1,)), ((), ())),
                    preferred_element_type=jnp.float32,
                ).reshape(GROUPS, rows, cache_len)
                scores = jnp.where(visible[None], scores, -jnp.inf)
                row_max = jnp.max(scores, axis=-1, keepdims=True)
                exponent = jnp.exp2((scores - row_max) * SCALE)
                row_total = jnp.sum(exponent, axis=-1, keepdims=True)
                weights = exponent.astype(jnp.bfloat16).reshape(GROUPS * rows, cache_len)
                mixed = jnp.dot(
                    weights,
                    block[:, (kv_heads + k) * HD : (kv_heads + k + 1) * HD],
                    preferred_element_type=jnp.float32,
                ).reshape(GROUPS, rows, HD)
                mixed = (mixed / row_total).astype(jnp.bfloat16)
                for g in range(GROUPS):
                    held[i, :, (head * GROUPS + g) * HD : (head * GROUPS + g + 1) * HD] = mixed[g]
        start = pl.multiple_of(where_ref[spot] * rows, rows)
        copy = pltpu.make_async_copy(held.at[i], out_ref.at[pl.ds(start, rows), :], sems.at[i])
        copy.start()
        copies.append(copy)
    for copy in copies:
        copy.wait()


def attend(prev, where, pos, queries, spots, blocks, first):
    rows = 16
    halves = len(blocks) // len(spots)
    width = queries.shape[1]
    vmem = pl.BlockSpec(memory_space=pltpu.VMEM)
    q_block = spots[0] // len(spots)
    body = functools.partial(attend_kernel, spots, halves)
    in_specs = [pl.BlockSpec(memory_space=pl.ANY), pl.BlockSpec(memory_space=pltpu.SMEM), vmem]
    in_specs += [pl.BlockSpec((rows * len(spots), width), lambda _: (q_block, 0))]
    in_specs += [pl.BlockSpec(b.shape, lambda _: (0, 0)) for b in blocks]
    args = [prev, where, pos, queries, *blocks]
    if first:
        del in_specs[0], args[0]
        inner = body

        def body(*refs):
            inner(None, *refs)

    cache_len = blocks[0].shape[0]
    work = rows * len(spots) * QH * cache_len
    return pl.pallas_call(
        body,
        grid=(1,),
        out_shape=jax.ShapeDtypeStruct(queries.shape, queries.dtype),
        in_specs=in_specs,
        out_specs=pl.BlockSpec(memory_space=pl.ANY),
        scratch_shapes=[
            pltpu.VMEM((len(spots), rows, width), jnp.bfloat16),
            pltpu.SemaphoreType.DMA((len(spots),)),
        ],
        input_output_aliases={} if first else {0: 0},
        compiler_params=pltpu.CompilerParams(vmem_limit_bytes=24 * 2**20),
        cost_estimate=pl.CostEstimate(
            flops=4 * work * HD, bytes_accessed=8 * 2**20, transcendentals=work
        ),
        name="attend_%d" % spots[0],
    )(*args)


def move_rows(targets, rows):
    count = rows.shape[0]
    pick = (jnp.arange(count, dtype=jnp.int32)[:, None] == targets[None, :]).astype(rows.dtype)
    return jnp.dot(pick, rows, preferred_element_type=jnp.float32).astype(rows.dtype)


def body(queries, send_list, recv_list, slot_pos, pack_seq, seq_kv):
    query_rows = queries[0, 0]
    row_count, width = query_rows.shape
    dp_count = lax.axis_size("dp")
    ring = lax.axis_size("prompt")
    group_rows = row_count // ring
    me = lax.axis_index("prompt")
    kv = seq_kv[0, 0]

    span = KVH * HD
    own = [
        jnp.concatenate([kv[:, lo : lo + span // 2], kv[:, span + lo : span + lo + span // 2]], axis=1)
        for lo in (0, span // 2)
    ]
    forward = [(i, (i + 1) % ring) for i in range(ring)]
    backward = [(i, (i - 1) % ring) for i in range(ring)]
    up, down = list(own), list(own)
    arrived_kv = []
    for step in range(ring // 2):
        for half in range(2):
            up[half] = lax.ppermute(up[half], "prompt", forward)
            if step < ring // 2 - 1:
                down[half] = lax.ppermute(down[half], "prompt", backward)
        arrived_kv.append((tuple(up), tuple(down)))

    ordered = move_rows(send_list[0, 0], query_rows)
    arrived = lax.all_to_all(
        ordered.reshape(dp_count, row_count // dp_count, width), "dp", split_axis=0, concat_axis=0, tiled=True
    ).reshape(row_count, width)

    sequences = pack_seq[0, 0]
    behind = (me - sequences) % ring
    half_way = ring // 2
    place = jnp.where(
        behind == 0,
        ring - 1,
        jnp.where(behind <= half_way, 2 * (behind - 1), 2 * (ring - behind - 1) + 1),
    )
    spots = jnp.arange(ring, dtype=jnp.int32)
    at_place = place[None, :] == spots[:, None]
    where = jnp.sum(jnp.where(at_place, spots[None, :], 0), axis=1)
    grouped_pos = slot_pos[0, 0].reshape(ring, group_rows)
    pos = jnp.sum(jnp.where(at_place[:, :, None], grouped_pos[None], 0), axis=1).T
    slot = recv_list[0, 0]
    of_group = (slot // group_rows)[:, None] == spots[None, :]
    target = jnp.sum(jnp.where(of_group, place[None, :], 0), axis=1) * group_rows + slot % group_rows
    packed = move_rows(target, arrived)

    out = attend(None, where, pos, packed, (ring - 1,), own, True)
    for step in range(ring // 2):
        up, down = arrived_kv[step]
        if step < ring // 2 - 1:
            out = attend(out, where, pos, packed, (2 * step, 2 * step + 1), (*up, *down), False)
        else:
            out = attend(out, where, pos, packed, (2 * step,), up, False)
    return out[None, None]


def solution(mesh):
    return jax.shard_map(
        body,
        mesh=mesh,
        in_specs=(
            P("prompt", "dp", None, None),
            P("prompt", "dp", None),
            P("prompt", "dp", None),
            P("prompt", "dp", None),
            P("prompt", "dp", None),
            P("dp", "prompt", None, None),
        ),
        out_specs=P("prompt", "dp", None, None),
        check_vma=False,
    )
```

```python
import functools
import math

import jax
import jax.numpy as jnp
from jax import lax
from jax.experimental import pallas as pl
from jax.experimental.pallas import tpu as pltpu
from jax.sharding import PartitionSpec as P

HD = 128
QH = 32
KVH = 4
GROUPS = QH // KVH
SCALE = math.log2(math.e) / math.sqrt(HD)


PARTS = 2
HEADS = KVH // PARTS


def score_group(query_ref, row, rows, blocks, limits, out_ref, out_row):
    cache_len = blocks[0].shape[0]
    visible = lax.broadcasted_iota(jnp.int32, (cache_len, GROUPS * rows), 0) <= limits
    for k in range(KVH):
        block, at = blocks[k // HEADS], k % HEADS
        heads = [slice((k * GROUPS + g) * HD, (k * GROUPS + g + 1) * HD) for g in range(GROUPS)]
        query = jnp.concatenate([query_ref[row : row + rows, h] for h in heads], axis=0)
        scores = lax.dot_general(
            block[:, at * HD : (at + 1) * HD],
            query,
            (((1,), (1,)), ((), ())),
            preferred_element_type=jnp.float32,
        )
        scores = jnp.where(visible, scores, -jnp.inf)
        row_max = jnp.max(scores, axis=0, keepdims=True)
        exponent = jnp.exp2((scores - row_max) * SCALE)
        row_total = jnp.sum(exponent, axis=0, keepdims=True)
        mixed = lax.dot_general(
            exponent.astype(jnp.bfloat16),
            block[:, (HEADS + at) * HD : (HEADS + at + 1) * HD],
            (((0,), (0,)), ((), ())),
            preferred_element_type=jnp.float32,
        )
        mixed = (mixed / row_total.reshape(GROUPS * rows, 1)).astype(jnp.bfloat16)
        for g in range(GROUPS):
            out_ref[out_row : out_row + rows, heads[g]] = mixed[g * rows : (g + 1) * rows]


def step_kernel(spots, rows, limits_ref, query_ref, *refs):
    blocks, out_ref = refs[:-1], refs[-1]
    for i, spot in enumerate(spots):
        group = blocks[PARTS * i : PARTS * (i + 1)]
        score_group(query_ref, spot * rows, rows, group, limits_ref[spot : spot + 1, :], out_ref, i * rows)


def guest_kernel(count, rows, *refs):
    blocks, refs = refs[:PARTS], refs[PARTS:]
    for guest_ref, out_ref in zip(refs[:count], refs[count:]):
        width = out_ref.shape[1]
        parts = guest_ref[:, width:].astype(jnp.float32)
        limits = (parts[0:1] * 16.0 + parts[1:2]).astype(jnp.int32)
        score_group(guest_ref, 0, rows, blocks, limits, out_ref, 0)


def place_kernel(ref_spots, rows, again, where_ref, *refs):
    if again:
        refs = refs[1:]
    held, out_ref, sems = refs[: len(ref_spots)], refs[-2], refs[-1]
    copies = []
    for ref, spots in zip(held, ref_spots):
        for i, spot in enumerate(spots):
            start = pl.multiple_of(where_ref[spot] * rows, rows)
            copy = pltpu.make_async_copy(
                ref.at[pl.ds(i * rows, rows), :], out_ref.at[pl.ds(start, rows), :], sems.at[len(copies)]
            )
            copy.start()
            copies.append(copy)
    for copy in copies:
        copy.wait()


def cost(spots, rows, cache_len):
    work = len(spots) * rows * QH * cache_len
    return pl.CostEstimate(flops=4 * work * HD, bytes_accessed=2**20, transcendentals=work)


VMEM = pl.BlockSpec(memory_space=pltpu.VMEM)
SMEM = pl.BlockSpec(memory_space=pltpu.SMEM)
ANY = pl.BlockSpec(memory_space=pl.ANY)
PARAMS = pltpu.CompilerParams(vmem_limit_bytes=10 * 2**20)


def attend_step(limits, packed, spots, blocks, rows):
    return pl.pallas_call(
        functools.partial(step_kernel, spots, rows),
        out_shape=jax.ShapeDtypeStruct((len(spots) * rows, packed.shape[1]), packed.dtype),
        in_specs=[VMEM] * (2 + len(blocks)),
        out_specs=VMEM,
        compiler_params=PARAMS,
        cost_estimate=cost(spots, rows, blocks[0].shape[0]),
        name="attend_%d" % spots[0],
    )(limits, packed, *blocks)


def attend_guests(guests, blocks, rows):
    width = guests[0].shape[1] - HD
    return pl.pallas_call(
        functools.partial(guest_kernel, len(guests), rows),
        out_shape=[jax.ShapeDtypeStruct((rows, width), g.dtype) for g in guests],
        in_specs=[VMEM] * (PARTS + len(guests)),
        out_specs=[VMEM] * len(guests),
        compiler_params=PARAMS,
        cost_estimate=cost(guests, rows, blocks[0].shape[0]),
        name="attend_guests",
    )(*blocks, *guests)


def place_rows(where, held, held_spots, rows, out, shape):
    again = out is not None
    return pl.pallas_call(
        functools.partial(place_kernel, tuple(held_spots), rows, again),
        out_shape=jax.ShapeDtypeStruct(shape, held[0].dtype),
        in_specs=[SMEM] + [ANY] * (again + len(held)),
        out_specs=ANY,
        scratch_shapes=[pltpu.SemaphoreType.DMA((sum(len(s) for s in held_spots),))],
        input_output_aliases={1: 0} if again else {},
        compiler_params=PARAMS,
        cost_estimate=pl.CostEstimate(flops=0, bytes_accessed=2 * held[0].size, transcendentals=0),
        name="place_last" if again else "place_held",
    )(where, *([out] if again else []), *held)


def move_rows(targets, rows):
    count = rows.shape[0]
    pick = (jnp.arange(count, dtype=jnp.int32)[:, None] == targets[None, :]).astype(rows.dtype)
    return jnp.dot(pick, rows, preferred_element_type=jnp.float32).astype(rows.dtype)


def tie(values, after):
    return lax.optimization_barrier((values, after))


def body(queries, send_list, recv_list, slot_pos, pack_seq, seq_kv):
    query_rows = queries[0, 0]
    row_count, width = query_rows.shape
    dp_count = lax.axis_size("dp")
    ring = lax.axis_size("prompt")
    group_rows = row_count // ring
    me = lax.axis_index("prompt")
    kv = seq_kv[0, 0]
    steps = ring // 2

    span, part = KVH * HD, HEADS * HD
    own = tuple(
        jnp.concatenate([kv[:, lo : lo + part], kv[:, span + lo : span + lo + part]], axis=1)
        for lo in range(0, span, part)
    )

    def shifted(x, by):
        return lax.ppermute(x, "prompt", [(i, (i + by) % ring) for i in range(ring)])

    def tie_first(parts, after):
        first, after = tie(parts[0], after)
        return (first, *parts[1:]), after

    up = tuple(shifted(x, 1) for x in own)
    down = tuple(shifted(x, -1) for x in own)
    blocks_of = [(*up, *down)]

    send, _ = tie(send_list[0, 0], up[0])
    ordered = move_rows(send, query_rows)
    arrived = lax.all_to_all(
        ordered.reshape(dp_count, row_count // dp_count, width), "dp", split_axis=0, concat_axis=0, tiled=True
    ).reshape(row_count, width)

    sequences = pack_seq[0, 0]
    behind = (me - sequences) % ring
    place = jnp.where(
        behind == 0,
        ring - 1,
        jnp.where(behind <= steps, 2 * (behind - 1), 2 * (ring - behind - 1) + 1),
    )
    spots = jnp.arange(ring, dtype=jnp.int32)
    at_place = place[None, :] == spots[:, None]
    where = jnp.sum(jnp.where(at_place, spots[None, :], 0), axis=1)
    grouped_pos = slot_pos[0, 0].reshape(ring, group_rows)
    limits = jnp.sum(jnp.where(at_place[:, :, None], grouped_pos[None], 0), axis=1)
    limits = jnp.tile(limits, (1, GROUPS))
    slot = recv_list[0, 0]
    of_group = (slot // group_rows)[:, None] == spots[None, :]
    target = jnp.sum(jnp.where(of_group, place[None, :], 0), axis=1) * group_rows + slot % group_rows
    packed = move_rows(target, arrived)

    far = steps - 2
    mine, behind_far, ahead_far, opposite = (ring - 1,), (2 * far,), (2 * far + 1,), (2 * far + 2,)

    def payload(spot):
        rows = packed[spot * group_rows : (spot + 1) * group_rows]
        parts = jnp.stack([limits[spot] // 16, limits[spot] % 16]).astype(rows.dtype)
        beside = jnp.pad(parts, ((0, group_rows - 2), (0, 0)))
        return jnp.concatenate([rows, beside], axis=1)

    held, held_spots = [], []

    def score(spot_list, blocks):
        held.append(attend_step(limits, packed, spot_list, blocks, group_rows))
        held_spots.append(spot_list)

    for step in range(1, far):
        if step == 2:
            up, ordered = tie_first(up, ordered)
        if step == 3:
            guests = [payload(s[0]) for s in (behind_far, opposite, ahead_far)]
            up, guests = tie_first(up, guests)
            guests = [shifted(g, by) for g, by in zip(guests, (-1, -2, 1))]
        if step == 4:
            score(mine, own)
            score((0, 1), blocks_of[0])
            up, (guests, held) = tie_first(up, (guests, held))
        if step == 5:
            score((2, 3), blocks_of[1])
            score((4, 5), blocks_of[2])
            up, held = tie_first(up, held)
        up = tuple(shifted(x, 1) for x in up)
        down = tuple(shifted(x, -1) for x in down)
        blocks_of.append((*up, *down))
    score((6, 7), blocks_of[3])
    score((8, 9), blocks_of[4])
    out = place_rows(where, held, held_spots, group_rows, None, packed.shape)
    up, out = tie_first(up, out)
    behind_out, opposite_out = attend_guests(guests[:2], up, group_rows)
    behind_out, opposite_out = shifted(behind_out, 1), shifted(opposite_out, 2)
    (ahead_out,) = attend_guests(guests[2:], down, group_rows)
    ahead_out = shifted(ahead_out, -1)
    held, held_spots = [], []
    score((2 * far - 2, 2 * far - 1), (*up, *down))
    out = place_rows(
        where,
        [*held, behind_out, opposite_out, ahead_out],
        [*held_spots, behind_far, opposite, ahead_far],
        group_rows,
        out,
        packed.shape,
    )
    return out[None, None]


def solution(mesh):
    return jax.shard_map(
        body,
        mesh=mesh,
        in_specs=(
            P("prompt", "dp", None, None),
            P("prompt", "dp", None),
            P("prompt", "dp", None),
            P("prompt", "dp", None),
            P("prompt", "dp", None),
            P("dp", "prompt", None, None),
        ),
        out_specs=P("prompt", "dp", None, None),
        check_vma=False,
    )
```

```python
import functools
import math

import jax
import jax.numpy as jnp
from jax import lax
from jax.experimental import pallas as pl
from jax.experimental.pallas import tpu as pltpu
from jax.sharding import PartitionSpec as P

HD = 128
QH = 32
KVH = 4
GROUPS = QH // KVH
SCALE = math.log2(math.e) / math.sqrt(HD)


def score_group(query_ref, row, rows, block, limits, out_ref, out_row):
    cache_len = block.shape[0]
    visible = lax.broadcasted_iota(jnp.int32, (cache_len, GROUPS * rows), 0) <= limits
    for k in range(KVH):
        heads = [slice((k * GROUPS + g) * HD, (k * GROUPS + g + 1) * HD) for g in range(GROUPS)]
        query = jnp.concatenate([query_ref[row : row + rows, h] for h in heads], axis=0)
        scores = lax.dot_general(
            block[:, k * HD : (k + 1) * HD],
            query,
            (((1,), (1,)), ((), ())),
            preferred_element_type=jnp.float32,
        )
        scores = jnp.where(visible, scores, -jnp.inf)
        row_max = jnp.max(scores, axis=0, keepdims=True)
        exponent = jnp.exp2((scores - row_max) * SCALE)
        row_total = jnp.sum(exponent, axis=0, keepdims=True)
        mixed = lax.dot_general(
            exponent.astype(jnp.bfloat16),
            block[:, (KVH + k) * HD : (KVH + k + 1) * HD],
            (((0,), (0,)), ((), ())),
            preferred_element_type=jnp.float32,
        )
        mixed = (mixed / row_total.reshape(GROUPS * rows, 1)).astype(jnp.bfloat16)
        for g in range(GROUPS):
            out_ref[out_row : out_row + rows, heads[g]] = mixed[g * rows : (g + 1) * rows]


def step_kernel(spots, rows, limits_ref, query_ref, *refs):
    blocks, out_ref = refs[:-1], refs[-1]
    for i, spot in enumerate(spots):
        score_group(query_ref, spot * rows, rows, blocks[i], limits_ref[spot : spot + 1, :], out_ref, i * rows)


def guest_kernel(count, rows, block, *refs):
    for guest_ref, out_ref in zip(refs[:count], refs[count:]):
        width = out_ref.shape[1]
        parts = guest_ref[:, width:].astype(jnp.float32)
        limits = (parts[0:1] * 16.0 + parts[1:2]).astype(jnp.int32)
        score_group(guest_ref, 0, rows, block, limits, out_ref, 0)


def place_kernel(ref_spots, rows, again, where_ref, *refs):
    if again:
        refs = refs[1:]
    held, out_ref, sems = refs[: len(ref_spots)], refs[-2], refs[-1]
    copies = []
    for ref, spots in zip(held, ref_spots):
        for i, spot in enumerate(spots):
            start = pl.multiple_of(where_ref[spot] * rows, rows)
            copy = pltpu.make_async_copy(
                ref.at[pl.ds(i * rows, rows), :], out_ref.at[pl.ds(start, rows), :], sems.at[len(copies)]
            )
            copy.start()
            copies.append(copy)
    for copy in copies:
        copy.wait()


def cost(spots, rows, cache_len):
    work = len(spots) * rows * QH * cache_len
    return pl.CostEstimate(flops=4 * work * HD, bytes_accessed=2**20, transcendentals=work)


VMEM = pl.BlockSpec(memory_space=pltpu.VMEM)
SMEM = pl.BlockSpec(memory_space=pltpu.SMEM)
ANY = pl.BlockSpec(memory_space=pl.ANY)
PARAMS = pltpu.CompilerParams(vmem_limit_bytes=10 * 2**20)


def attend_step(limits, packed, spots, blocks, rows):
    return pl.pallas_call(
        functools.partial(step_kernel, spots, rows),
        out_shape=jax.ShapeDtypeStruct((len(spots) * rows, packed.shape[1]), packed.dtype),
        in_specs=[VMEM] * (2 + len(spots)),
        out_specs=VMEM,
        compiler_params=PARAMS,
        cost_estimate=cost(spots, rows, blocks[0].shape[0]),
        name="attend_%d" % spots[0],
    )(limits, packed, *blocks)


def attend_guests(guests, block, rows):
    width = guests[0].shape[1] - HD
    return pl.pallas_call(
        functools.partial(guest_kernel, len(guests), rows),
        out_shape=[jax.ShapeDtypeStruct((rows, width), g.dtype) for g in guests],
        in_specs=[VMEM] * (1 + len(guests)),
        out_specs=[VMEM] * len(guests),
        compiler_params=PARAMS,
        cost_estimate=cost(guests, rows, block.shape[0]),
        name="attend_guests",
    )(block, *guests)


def place_rows(where, held, held_spots, rows, out, shape):
    again = out is not None
    return pl.pallas_call(
        functools.partial(place_kernel, tuple(held_spots), rows, again),
        out_shape=jax.ShapeDtypeStruct(shape, held[0].dtype),
        in_specs=[SMEM] + [ANY] * (again + len(held)),
        out_specs=ANY,
        scratch_shapes=[pltpu.SemaphoreType.DMA((sum(len(s) for s in held_spots),))],
        input_output_aliases={1: 0} if again else {},
        compiler_params=PARAMS,
        cost_estimate=pl.CostEstimate(flops=0, bytes_accessed=2 * held[0].size, transcendentals=0),
        name="place_last" if again else "place_held",
    )(where, *([out] if again else []), *held)


def move_rows(targets, rows):
    count = rows.shape[0]
    pick = (jnp.arange(count, dtype=jnp.int32)[:, None] == targets[None, :]).astype(rows.dtype)
    return jnp.dot(pick, rows, preferred_element_type=jnp.float32).astype(rows.dtype)


def tie(values, after):
    return lax.optimization_barrier((values, after))


def body(queries, send_list, recv_list, slot_pos, pack_seq, seq_kv):
    query_rows = queries[0, 0]
    row_count, width = query_rows.shape
    dp_count = lax.axis_size("dp")
    ring = lax.axis_size("prompt")
    group_rows = row_count // ring
    me = lax.axis_index("prompt")
    kv = seq_kv[0, 0]

    def shifted(x, by):
        return lax.ppermute(x, "prompt", [(i, (i + by) % ring) for i in range(ring)])

    steps = ring // 2

    ordered = move_rows(send_list[0, 0], query_rows)
    arrived = lax.all_to_all(
        ordered.reshape(dp_count, row_count // dp_count, width), "dp", split_axis=0, concat_axis=0, tiled=True
    ).reshape(row_count, width)

    sequences = pack_seq[0, 0]
    offset = (me - sequences) % ring
    place = jnp.where(
        offset == 0,
        ring - 1,
        jnp.where(offset <= steps, 2 * (offset - 1), 2 * (ring - offset - 1) + 1),
    )
    spots = jnp.arange(ring, dtype=jnp.int32)
    at_place = place[None, :] == spots[:, None]
    where = jnp.sum(jnp.where(at_place, spots[None, :], 0), axis=1)
    grouped_pos = slot_pos[0, 0].reshape(ring, group_rows)
    limits = jnp.sum(jnp.where(at_place[:, :, None], grouped_pos[None], 0), axis=1)
    limits = jnp.tile(limits, (1, GROUPS))
    slot = recv_list[0, 0]
    of_group = (slot // group_rows)[:, None] == spots[None, :]
    target = jnp.sum(jnp.where(of_group, place[None, :], 0), axis=1) * group_rows + slot % group_rows
    packed = move_rows(target, arrived)

    far = steps - 4
    behind = [2 * (d - 1) for d in range(steps, far, -1)]
    ahead = [2 * (d - 1) + 1 for d in range(steps - 1, far, -1)]
    behind_hops = [d - far for d in range(steps, far, -1)]
    ahead_hops = [d - far for d in range(steps - 1, far, -1)]

    def payload(spot):
        rows = packed[spot * group_rows : (spot + 1) * group_rows]
        parts = jnp.stack([limits[spot] // 16, limits[spot] % 16]).astype(rows.dtype)
        beside = jnp.pad(parts, ((0, group_rows - 2), (0, 0)))
        return jnp.concatenate([rows, beside], axis=1)

    held, held_spots = [], []

    def score(spot_list, blocks):
        held.append(attend_step(limits, packed, spot_list, blocks, group_rows))
        held_spots.append(spot_list)

    up, down = kv, kv
    blocks_of = []
    for step in range(far):
        if step == 0:
            down, ordered = tie(down, ordered)
        if step == far - 2:
            from_behind, from_ahead = [payload(s) for s in behind], [payload(s) for s in ahead]
            up, (from_behind, from_ahead) = tie(up, (from_behind, from_ahead))
            from_behind = [shifted(g, -by) for g, by in zip(from_behind, behind_hops)]
            from_ahead = [shifted(g, by) for g, by in zip(from_ahead, ahead_hops)]
        if step == far - 1:
            score((ring - 1,), (kv,))
            score((0, 1), blocks_of[0])
            up, (held, from_behind) = tie(up, (held, from_behind))
        up = shifted(up, 1)
        down = shifted(down, -1)
        blocks_of.append((up, down))
    for step in range(1, far - 1):
        score((2 * step, 2 * step + 1), blocks_of[step])
    out = place_rows(where, held, held_spots, group_rows, None, packed.shape)
    up, out = tie(up, out)
    from_behind = attend_guests(from_behind, up, group_rows)
    from_behind = [shifted(g, by) for g, by in zip(from_behind, behind_hops)]
    from_ahead = attend_guests(from_ahead, down, group_rows)
    from_ahead = [shifted(g, -by) for g, by in zip(from_ahead, ahead_hops)]
    held, held_spots = [], []
    score((2 * far - 2, 2 * far - 1), (up, down))
    out = place_rows(
        where,
        [*held, *from_behind, *from_ahead],
        [*held_spots, *((s,) for s in behind), *((s,) for s in ahead)],
        group_rows,
        out,
        packed.shape,
    )
    return out[None, None]


def solution(mesh):
    return jax.shard_map(
        body,
        mesh=mesh,
        in_specs=(
            P("prompt", "dp", None, None),
            P("prompt", "dp", None),
            P("prompt", "dp", None),
            P("prompt", "dp", None),
            P("prompt", "dp", None),
            P("dp", "prompt", None, None),
        ),
        out_specs=P("prompt", "dp", None, None),
        check_vma=False,
    )
```

```python
import functools
import math

import jax
import jax.numpy as jnp
from jax import lax
from jax.experimental import pallas as pl
from jax.experimental.pallas import tpu as pltpu
from jax.sharding import PartitionSpec as P

HD = 128
QH = 32
KVH = 4
GROUPS = QH // KVH
SCALE = math.log2(math.e) / math.sqrt(HD)


def score_group(query_ref, row, rows, block, limits, out_ref, out_row):
    cache_len = block.shape[0]
    visible = lax.broadcasted_iota(jnp.int32, (cache_len, GROUPS * rows), 0) <= limits
    for k in range(KVH):
        heads = [slice((k * GROUPS + g) * HD, (k * GROUPS + g + 1) * HD) for g in range(GROUPS)]
        query = jnp.concatenate([query_ref[row : row + rows, h] for h in heads], axis=0)
        scores = lax.dot_general(
            block[:, k * HD : (k + 1) * HD],
            query,
            (((1,), (1,)), ((), ())),
            preferred_element_type=jnp.float32,
        )
        scores = jnp.where(visible, scores, -jnp.inf)
        row_max = jnp.max(scores, axis=0, keepdims=True)
        exponent = jnp.exp2((scores - row_max) * SCALE)
        row_total = jnp.sum(exponent, axis=0, keepdims=True)
        mixed = lax.dot_general(
            exponent.astype(jnp.bfloat16),
            block[:, (KVH + k) * HD : (KVH + k + 1) * HD],
            (((0,), (0,)), ((), ())),
            preferred_element_type=jnp.float32,
        )
        mixed = (mixed / row_total.reshape(GROUPS * rows, 1)).astype(jnp.bfloat16)
        for g in range(GROUPS):
            out_ref[out_row : out_row + rows, heads[g]] = mixed[g * rows : (g + 1) * rows]


def step_kernel(spots, rows, limits_ref, query_ref, *refs):
    blocks, out_ref = refs[:-1], refs[-1]
    for i, spot in enumerate(spots):
        score_group(query_ref, spot * rows, rows, blocks[i], limits_ref[spot : spot + 1, :], out_ref, i * rows)


def guest_kernel(sources, rows, *refs):
    count = len(sources)
    blocks, guests, outs = refs[: -2 * count], refs[-2 * count : -count], refs[-count:]
    for source, guest_ref, out_ref in zip(sources, guests, outs):
        width = out_ref.shape[1]
        parts = guest_ref[:, width:].astype(jnp.float32)
        limits = (parts[0:1] * 16.0 + parts[1:2]).astype(jnp.int32)
        score_group(guest_ref, 0, rows, blocks[source], limits, out_ref, 0)


def place_kernel(ref_spots, rows, again, where_ref, *refs):
    if again:
        refs = refs[1:]
    held, out_ref, sems = refs[: len(ref_spots)], refs[-2], refs[-1]
    copies = []
    for ref, spots in zip(held, ref_spots):
        for i, spot in enumerate(spots):
            start = pl.multiple_of(where_ref[spot] * rows, rows)
            copy = pltpu.make_async_copy(
                ref.at[pl.ds(i * rows, rows), :], out_ref.at[pl.ds(start, rows), :], sems.at[len(copies)]
            )
            copy.start()
            copies.append(copy)
    for copy in copies:
        copy.wait()


def cost(spots, rows, cache_len):
    work = len(spots) * rows * QH * cache_len
    return pl.CostEstimate(flops=4 * work * HD, bytes_accessed=2**20, transcendentals=work)


VMEM = pl.BlockSpec(memory_space=pltpu.VMEM)
SMEM = pl.BlockSpec(memory_space=pltpu.SMEM)
ANY = pl.BlockSpec(memory_space=pl.ANY)
PARAMS = pltpu.CompilerParams(vmem_limit_bytes=10 * 2**20)


def attend_step(limits, packed, spots, blocks, rows):
    return pl.pallas_call(
        functools.partial(step_kernel, spots, rows),
        out_shape=jax.ShapeDtypeStruct((len(spots) * rows, packed.shape[1]), packed.dtype),
        in_specs=[VMEM] * (2 + len(spots)),
        out_specs=VMEM,
        compiler_params=PARAMS,
        cost_estimate=cost(spots, rows, blocks[0].shape[0]),
        name="attend_%d" % spots[0],
    )(limits, packed, *blocks)


def attend_guests(guests, sources, blocks, rows):
    width = guests[0].shape[1] - HD
    return pl.pallas_call(
        functools.partial(guest_kernel, sources, rows),
        out_shape=[jax.ShapeDtypeStruct((rows, width), g.dtype) for g in guests],
        in_specs=[VMEM] * (len(blocks) + len(guests)),
        out_specs=[VMEM] * len(guests),
        compiler_params=PARAMS,
        cost_estimate=cost(guests, rows, blocks[0].shape[0]),
        name="attend_guests",
    )(*blocks, *guests)


def place_rows(where, held, held_spots, rows, out, shape):
    again = out is not None
    return pl.pallas_call(
        functools.partial(place_kernel, tuple(held_spots), rows, again),
        out_shape=jax.ShapeDtypeStruct(shape, held[0].dtype),
        in_specs=[SMEM] + [ANY] * (again + len(held)),
        out_specs=ANY,
        scratch_shapes=[pltpu.SemaphoreType.DMA((sum(len(s) for s in held_spots),))],
        input_output_aliases={1: 0} if again else {},
        compiler_params=PARAMS,
        cost_estimate=pl.CostEstimate(flops=0, bytes_accessed=2 * held[0].size, transcendentals=0),
        name="place_last" if again else "place_held",
    )(where, *([out] if again else []), *held)


def move_rows(targets, rows):
    count = rows.shape[0]
    pick = (jnp.arange(count, dtype=jnp.int32)[:, None] == targets[None, :]).astype(rows.dtype)
    return jnp.dot(pick, rows, preferred_element_type=jnp.float32).astype(rows.dtype)


def tie(values, after):
    return lax.optimization_barrier((values, after))


def body(queries, send_list, recv_list, slot_pos, pack_seq, seq_kv):
    query_rows = queries[0, 0]
    row_count, width = query_rows.shape
    dp_count = lax.axis_size("dp")
    ring = lax.axis_size("prompt")
    group_rows = row_count // ring
    me = lax.axis_index("prompt")
    kv = seq_kv[0, 0]

    def shifted(x, by):
        return lax.ppermute(x, "prompt", [(i, (i + by) % ring) for i in range(ring)])

    steps = ring // 2

    ordered = move_rows(send_list[0, 0], query_rows)
    arrived = lax.all_to_all(
        ordered.reshape(dp_count, row_count // dp_count, width), "dp", split_axis=0, concat_axis=0, tiled=True
    ).reshape(row_count, width)

    sequences = pack_seq[0, 0]
    behind = (me - sequences) % ring
    place = jnp.where(
        behind == 0,
        ring - 1,
        jnp.where(behind <= steps, 2 * (behind - 1), 2 * (ring - behind - 1) + 1),
    )
    spots = jnp.arange(ring, dtype=jnp.int32)
    at_place = place[None, :] == spots[:, None]
    where = jnp.sum(jnp.where(at_place, spots[None, :], 0), axis=1)
    grouped_pos = slot_pos[0, 0].reshape(ring, group_rows)
    limits = jnp.sum(jnp.where(at_place[:, :, None], grouped_pos[None], 0), axis=1)
    limits = jnp.tile(limits, (1, GROUPS))
    slot = recv_list[0, 0]
    of_group = (slot // group_rows)[:, None] == spots[None, :]
    target = jnp.sum(jnp.where(of_group, place[None, :], 0), axis=1) * group_rows + slot % group_rows
    packed = move_rows(target, arrived)

    far = steps - 2
    mine, behind_far, ahead_far, opposite = (ring - 1,), (2 * far,), (2 * far + 1,), (2 * far + 2,)

    def payload(spot):
        rows = packed[spot * group_rows : (spot + 1) * group_rows]
        parts = jnp.stack([limits[spot] // 16, limits[spot] % 16]).astype(rows.dtype)
        beside = jnp.pad(parts, ((0, group_rows - 2), (0, 0)))
        return jnp.concatenate([rows, beside], axis=1)

    up, down = kv, kv
    held, held_spots = [], []
    blocks_of = []

    def score(spot_list, blocks):
        held.append(attend_step(limits, packed, spot_list, blocks, group_rows))
        held_spots.append(spot_list)

    for step in range(far):
        if step == 2:
            up, ordered = tie(up, ordered)
        if step == 3:
            guests = [payload(s[0]) for s in (opposite, behind_far, ahead_far)]
            up, guests = tie(up, guests)
            guests = [shifted(g, by) for g, by in zip(guests, (-2, -1, 1))]
        if step == 4:
            score(mine, (kv,))
            score((0, 1), blocks_of[0])
            up, (guests, held) = tie(up, (guests, held))
        if step == 5:
            score((2, 3), blocks_of[1])
            score((4, 5), blocks_of[2])
            up, held = tie(up, held)
        up = shifted(up, 1)
        down = shifted(down, -1)
        blocks_of.append((up, down))
    score((6, 7), blocks_of[3])
    score((8, 9), blocks_of[4])
    out = place_rows(where, held, held_spots, group_rows, None, packed.shape)
    up, out = tie(up, out)
    back = attend_guests(guests, (0, 0, 1), (up, down), group_rows)
    back = [shifted(g, by) for g, by in zip(back, (2, 1, -1))]
    held, held_spots = [], []
    score((2 * far - 2, 2 * far - 1), (up, down))
    out = place_rows(
        where, [*held, *back], [*held_spots, opposite, behind_far, ahead_far], group_rows, out, packed.shape
    )
    return out[None, None]


def solution(mesh):
    return jax.shard_map(
        body,
        mesh=mesh,
        in_specs=(
            P("prompt", "dp", None, None),
            P("prompt", "dp", None),
            P("prompt", "dp", None),
            P("prompt", "dp", None),
            P("prompt", "dp", None),
            P("dp", "prompt", None, None),
        ),
        out_specs=P("prompt", "dp", None, None),
        check_vma=False,
    )
```

```python
import functools
import math

import jax
import jax.numpy as jnp
from jax import lax
from jax.experimental import pallas as pl
from jax.experimental.pallas import tpu as pltpu
from jax.sharding import PartitionSpec as P

HD = 128
QH = 32
KVH = 4
GROUPS = QH // KVH
SCALE = math.log2(math.e) / math.sqrt(HD)


HALF = KVH // 2


def score_group(query_ref, row, rows, block, limits, out_ref, out_row):
    cache_len = block.shape[0]
    visible = lax.broadcasted_iota(jnp.int32, (cache_len, GROUPS * rows), 0) <= limits
    for k in range(HALF):
        heads = [slice((k * GROUPS + g) * HD, (k * GROUPS + g + 1) * HD) for g in range(GROUPS)]
        query = jnp.concatenate([query_ref[row : row + rows, h] for h in heads], axis=0)
        scores = lax.dot_general(
            block[:, k * HD : (k + 1) * HD],
            query,
            (((1,), (1,)), ((), ())),
            preferred_element_type=jnp.float32,
        )
        scores = jnp.where(visible, scores, -jnp.inf)
        row_max = jnp.max(scores, axis=0, keepdims=True)
        exponent = jnp.exp2((scores - row_max) * SCALE)
        row_total = jnp.sum(exponent, axis=0, keepdims=True)
        mixed = lax.dot_general(
            exponent.astype(jnp.bfloat16),
            block[:, (HALF + k) * HD : (HALF + k + 1) * HD],
            (((0,), (0,)), ((), ())),
            preferred_element_type=jnp.float32,
        )
        mixed = (mixed / row_total.reshape(GROUPS * rows, 1)).astype(jnp.bfloat16)
        for g in range(GROUPS):
            out_ref[out_row : out_row + rows, heads[g]] = mixed[g * rows : (g + 1) * rows]


def step_kernel(spots, rows, limits_ref, query_ref, *refs):
    blocks, out_ref = refs[:-1], refs[-1]
    for i, spot in enumerate(spots):
        score_group(query_ref, spot * rows, rows, blocks[i], limits_ref[spot : spot + 1, :], out_ref, i * rows)


def guest_kernel(sources, rows, *refs):
    count = len(sources)
    blocks, guests, outs = refs[: -2 * count], refs[-2 * count : -count], refs[-count:]
    for source, guest_ref, out_ref in zip(sources, guests, outs):
        width = out_ref.shape[1]
        parts = guest_ref[:, width:].astype(jnp.float32)
        limits = (parts[0:1] * 16.0 + parts[1:2]).astype(jnp.int32)
        score_group(guest_ref, 0, rows, blocks[source], limits, out_ref, 0)


def place_kernel(ref_spots, rows, again, where_ref, *refs):
    if again:
        refs = refs[1:]
    held, out_ref, sems = refs[: len(ref_spots)], refs[-2], refs[-1]
    copies = []
    width = held[0].shape[1]
    for ref, spots in zip(held, ref_spots):
        for i, spot in enumerate(spots):
            start = pl.multiple_of(where_ref[spot] * rows, rows)
            copy = pltpu.make_async_copy(
                ref.at[pl.ds(i * rows, rows), :], out_ref.at[pl.ds(start, rows), pl.ds(width, width)], sems.at[len(copies)]
            )
            copy.start()
            copies.append(copy)
    for copy in copies:
        copy.wait()


def gathered_kernel(rows, place_ref, seq_ref, prev_ref, limits_ref, query_a, query_b, block_a, block_b, out_ref):
    del seq_ref, prev_ref
    for i, (query_ref, block) in enumerate(((query_a, block_a), (query_b, block_b))):
        spot = place_ref[2 * pl.program_id(0) + i]
        score_group(query_ref, 0, rows, block.at[0], limits_ref[pl.ds(spot, 1), :], out_ref, i * rows)


def cost(spots, rows, cache_len):
    work = len(spots) * rows * QH * cache_len
    return pl.CostEstimate(flops=4 * work * HD, bytes_accessed=2**20, transcendentals=work)


VMEM = pl.BlockSpec(memory_space=pltpu.VMEM)
SMEM = pl.BlockSpec(memory_space=pltpu.SMEM)
ANY = pl.BlockSpec(memory_space=pl.ANY)
PARAMS = pltpu.CompilerParams(vmem_limit_bytes=10 * 2**20)


def attend_step(limits, packed, spots, blocks, rows):
    return pl.pallas_call(
        functools.partial(step_kernel, spots, rows),
        out_shape=jax.ShapeDtypeStruct((len(spots) * rows, packed.shape[1]), packed.dtype),
        in_specs=[VMEM] * (2 + len(spots)),
        out_specs=VMEM,
        compiler_params=PARAMS,
        cost_estimate=cost(spots, rows, blocks[0].shape[0]),
        name="attend_%d" % spots[0],
    )(limits, packed, *blocks)


def attend_guests(guests, sources, blocks, rows):
    width = guests[0].shape[1] - HD
    return pl.pallas_call(
        functools.partial(guest_kernel, sources, rows),
        out_shape=[jax.ShapeDtypeStruct((rows, width), g.dtype) for g in guests],
        in_specs=[VMEM] * (len(blocks) + len(guests)),
        out_specs=[VMEM] * len(guests),
        compiler_params=PARAMS,
        cost_estimate=cost(guests, rows, blocks[0].shape[0]),
        name="attend_guests",
    )(*blocks, *guests)


def place_rows(where, held, held_spots, rows, out, shape):
    again = out is not None
    return pl.pallas_call(
        functools.partial(place_kernel, tuple(held_spots), rows, again),
        out_shape=jax.ShapeDtypeStruct(shape, held[0].dtype),
        in_specs=[SMEM] + [ANY] * (again + len(held)),
        out_specs=ANY,
        scratch_shapes=[pltpu.SemaphoreType.DMA((sum(len(s) for s in held_spots),))],
        input_output_aliases={1: 0} if again else {},
        compiler_params=PARAMS,
        cost_estimate=pl.CostEstimate(flops=0, bytes_accessed=2 * held[0].size, transcendentals=0),
        name="place_last" if again else "place_held",
    )(where, *([out] if again else []), *held)


def attend_gathered(place, sequences, limits, packed, gathered, out, rows):
    count, cache_len, span = gathered.shape
    width = packed.shape[1]

    def query_spec(i):
        return pl.BlockSpec((rows, width), lambda g, place, seq: (place[2 * g + i], 0))

    def block_spec(i):
        return pl.BlockSpec((1, cache_len, span), lambda g, place, seq: (seq[2 * g + i], 0, 0))

    return pl.pallas_call(
        functools.partial(gathered_kernel, rows),
        out_shape=jax.ShapeDtypeStruct(out.shape, out.dtype),
        grid_spec=pltpu.PrefetchScalarGridSpec(
            num_scalar_prefetch=2,
            grid=(count // 2,),
            in_specs=[
                ANY,
                pl.BlockSpec(limits.shape, lambda g, place, seq: (0, 0)),
                query_spec(0),
                query_spec(1),
                block_spec(0),
                block_spec(1),
            ],
            out_specs=pl.BlockSpec((2 * rows, width), lambda g, place, seq: (g, 0)),
        ),
        input_output_aliases={2: 0},
        compiler_params=PARAMS,
        cost_estimate=pl.CostEstimate(
            flops=2 * count * rows * QH * cache_len * HD,
            bytes_accessed=2 * gathered.size + 4 * packed.size,
            transcendentals=count * rows * QH * cache_len // 2,
        ),
        name="attend_gathered",
    )(place, sequences, out, limits, packed, packed, gathered, gathered)


def move_rows(targets, rows):
    count = rows.shape[0]
    pick = (jnp.arange(count, dtype=jnp.int32)[:, None] == targets[None, :]).astype(rows.dtype)
    return jnp.dot(pick, rows, preferred_element_type=jnp.float32).astype(rows.dtype)


def tie(values, after):
    return lax.optimization_barrier((values, after))


def body(queries, send_list, recv_list, slot_pos, pack_seq, seq_kv):
    query_rows = queries[0, 0]
    row_count, width = query_rows.shape
    dp_count = lax.axis_size("dp")
    ring = lax.axis_size("prompt")
    group_rows = row_count // ring
    me = lax.axis_index("prompt")
    kv = seq_kv[0, 0]

    def shifted(x, by):
        return lax.ppermute(x, "prompt", [(i, (i + by) % ring) for i in range(ring)])

    steps = ring // 2

    span, half = KVH * HD, HALF * HD
    first_half, second_half = (
        jnp.concatenate([kv[:, lo : lo + half], kv[:, span + lo : span + lo + half]], axis=1) for lo in (0, half)
    )
    gathered = lax.all_gather(first_half, "prompt", axis=0)

    ordered = move_rows(send_list[0, 0], query_rows)
    arrived = lax.all_to_all(
        ordered.reshape(dp_count, row_count // dp_count, width), "dp", split_axis=0, concat_axis=0, tiled=True
    ).reshape(row_count, width)

    sequences = pack_seq[0, 0]
    behind = (me - sequences) % ring
    place = jnp.where(
        behind == 0,
        ring - 1,
        jnp.where(behind <= steps, 2 * (behind - 1), 2 * (ring - behind - 1) + 1),
    )
    spots = jnp.arange(ring, dtype=jnp.int32)
    at_place = place[None, :] == spots[:, None]
    where = jnp.sum(jnp.where(at_place, spots[None, :], 0), axis=1)
    grouped_pos = slot_pos[0, 0].reshape(ring, group_rows)
    limits = jnp.sum(jnp.where(at_place[:, :, None], grouped_pos[None], 0), axis=1)
    limits = jnp.tile(limits, (1, GROUPS))
    slot = recv_list[0, 0]
    of_group = (slot // group_rows)[:, None] == spots[None, :]
    target = jnp.sum(jnp.where(of_group, place[None, :], 0), axis=1) * group_rows + slot % group_rows
    packed_first = move_rows(target, arrived[:, : width // 2])
    packed = move_rows(target, arrived[:, width // 2 :])

    far = steps - 2
    mine, behind_far, ahead_far, opposite = (ring - 1,), (2 * far,), (2 * far + 1,), (2 * far + 2,)

    def payload(spot):
        rows = packed[spot * group_rows : (spot + 1) * group_rows]
        parts = jnp.stack([limits[spot] // 16, limits[spot] % 16]).astype(rows.dtype)
        beside = jnp.pad(parts, ((0, group_rows - 2), (0, 0)))
        return jnp.concatenate([rows, beside], axis=1)

    up, down = second_half, second_half
    held, held_spots = [], []
    blocks_of = []

    def score(spot_list, blocks):
        held.append(attend_step(limits, packed, spot_list, blocks, group_rows))
        held_spots.append(spot_list)

    for step in range(far):
        if step == 2:
            up, ordered = tie(up, ordered)
        if step == 3:
            guests = [payload(s[0]) for s in (opposite, behind_far, ahead_far)]
            up, guests = tie(up, guests)
            guests = [shifted(g, by) for g, by in zip(guests, (-2, -1, 1))]
        if step == 4:
            score(mine, (second_half,))
            score((0, 1), blocks_of[0])
            up, (guests, held) = tie(up, (guests, held))
        if step == 5:
            score((2, 3), blocks_of[1])
            score((4, 5), blocks_of[2])
            up, held = tie(up, held)
        up = shifted(up, 1)
        down = shifted(down, -1)
        blocks_of.append((up, down))
    score((6, 7), blocks_of[3])
    score((8, 9), blocks_of[4])
    out = place_rows(where, held, held_spots, group_rows, None, query_rows.shape)
    up, out = tie(up, out)
    back = attend_guests(guests, (0, 0, 1), (up, down), group_rows)
    out, back = tie(out, back)
    back = [shifted(g, by) for g, by in zip(back, (2, 1, -1))]
    out = attend_gathered(place, sequences, limits, packed_first, gathered, out, group_rows)
    held, held_spots = [], []
    score((2 * far - 2, 2 * far - 1), (up, down))
    out = place_rows(
        where, [*held, *back], [*held_spots, opposite, behind_far, ahead_far], group_rows, out, query_rows.shape
    )
    return out[None, None]


def solution(mesh):
    return jax.shard_map(
        body,
        mesh=mesh,
        in_specs=(
            P("prompt", "dp", None, None),
            P("prompt", "dp", None),
            P("prompt", "dp", None),
            P("prompt", "dp", None),
            P("prompt", "dp", None),
            P("dp", "prompt", None, None),
        ),
        out_specs=P("prompt", "dp", None, None),
        check_vma=False,
    )
```

```python
import functools
import math

import jax
import jax.numpy as jnp
from jax import lax
from jax.experimental import pallas as pl
from jax.experimental.pallas import tpu as pltpu
from jax.sharding import PartitionSpec as P

HD = 128
QH = 32
KVH = 4
GROUPS = QH // KVH
SCALE = math.log2(math.e) / math.sqrt(HD)


HALF = KVH // 2


def head_of(parts, k):
    kind, refs = parts
    at, half = k % HALF, k // HALF
    if kind == "cached":
        return refs[0], k * HD, (KVH + k) * HD
    if kind == "halves":
        return refs[half], at * HD, (HALF + at) * HD
    return refs[0], (2 * half * HALF + at) * HD, ((2 * half + 1) * HALF + at) * HD


def score_group(query_of, rows, parts, cache_len, limits, out_ref, out_row):
    visible = lax.broadcasted_iota(jnp.int32, (cache_len, GROUPS * rows), 0) <= limits
    for k in range(KVH):
        block, key_at, value_at = head_of(parts, k)
        query = jnp.concatenate([query_of(k, g) for g in range(GROUPS)], axis=0)
        scores = lax.dot_general(
            block[:cache_len, key_at : key_at + HD],
            query,
            (((1,), (1,)), ((), ())),
            preferred_element_type=jnp.float32,
        )
        scores = jnp.where(visible, scores, -jnp.inf)
        row_max = jnp.max(scores, axis=0, keepdims=True)
        exponent = jnp.exp2((scores - row_max) * SCALE)
        row_total = jnp.sum(exponent, axis=0, keepdims=True)
        mixed = lax.dot_general(
            exponent.astype(jnp.bfloat16),
            block[:cache_len, value_at : value_at + HD],
            (((0,), (0,)), ((), ())),
            preferred_element_type=jnp.float32,
        )
        mixed = (mixed / row_total.reshape(GROUPS * rows, 1)).astype(jnp.bfloat16)
        for g in range(GROUPS):
            column = (k * GROUPS + g) * HD
            out_ref[out_row : out_row + rows, column : column + HD] = mixed[g * rows : (g + 1) * rows]


def take(kinds, refs):
    refs, blocks = list(refs), []
    for kind in kinds:
        count = 2 if kind == "halves" else 1
        blocks.append((kind, refs[:count]))
        del refs[:count]
    return blocks


def step_kernel(spots, kinds, rows, cache_len, limits_ref, query_ref, *refs):
    blocks, out_ref = take(kinds, refs[:-1]), refs[-1]
    for i, spot in enumerate(spots):

        def query_of(k, g, row=spot * rows):
            return query_ref[row : row + rows, (k * GROUPS + g) * HD : (k * GROUPS + g + 1) * HD]

        score_group(query_of, rows, blocks[i], cache_len, limits_ref[spot : spot + 1, :], out_ref, i * rows)


def guest_kernel(count, rows, cache_len, block, *refs):
    for guest_ref, out_ref in zip(refs[:count], refs[count:]):
        places = guest_ref[KVH * rows : (KVH + 1) * rows, :HD].astype(jnp.float32)
        limits = (places[0:1] * 16.0 + places[1:2]).astype(jnp.int32)

        def query_of(k, g, guest_ref=guest_ref):
            return guest_ref[k * rows : (k + 1) * rows, g * HD : (g + 1) * HD]

        score_group(query_of, rows, ("joined", [block]), cache_len, limits, out_ref, 0)


def place_kernel(ref_spots, rows, again, where_ref, *refs):
    if again:
        refs = refs[1:]
    held, out_ref, sems = refs[: len(ref_spots)], refs[-2], refs[-1]
    copies = []
    for ref, spots in zip(held, ref_spots):
        for i, spot in enumerate(spots):
            start = pl.multiple_of(where_ref[spot] * rows, rows)
            copy = pltpu.make_async_copy(
                ref.at[pl.ds(i * rows, rows), :], out_ref.at[pl.ds(start, rows), :], sems.at[len(copies)]
            )
            copy.start()
            copies.append(copy)
    for copy in copies:
        copy.wait()


def join_kernel(spots, rows, limits_ref, query_ref, first_ref, second_ref, out_ref):
    cache_len, width = first_ref.shape
    out_ref[:cache_len, :width] = first_ref[...]
    out_ref[:cache_len, width:] = second_ref[...]
    for i, spot in enumerate(spots):
        base = cache_len + i * (KVH + 1) * rows
        for k in range(KVH):
            heads = query_ref[spot * rows : (spot + 1) * rows, 2 * k * width : 2 * (k + 1) * width]
            out_ref[base + k * rows : base + (k + 1) * rows, :] = heads
        places = jnp.broadcast_to(limits_ref[spot : spot + 1, :], (rows, limits_ref.shape[1]))
        row = lax.broadcasted_iota(jnp.int32, places.shape, 0)
        places = jnp.where(row == 0, places >> 4, jnp.where(row == 1, places & 15, 0))
        below = base + KVH * rows
        out_ref[below : below + rows, :] = jnp.zeros((rows, 2 * width), out_ref.dtype)
        out_ref[below : below + rows, : places.shape[1]] = places.astype(jnp.float32).astype(out_ref.dtype)


def cost(spots, rows, cache_len):
    work = len(spots) * rows * QH * cache_len
    return pl.CostEstimate(flops=4 * work * HD, bytes_accessed=2**20, transcendentals=work)


VMEM = pl.BlockSpec(memory_space=pltpu.VMEM)
SMEM = pl.BlockSpec(memory_space=pltpu.SMEM)
ANY = pl.BlockSpec(memory_space=pl.ANY)
PARAMS = pltpu.CompilerParams(vmem_limit_bytes=10 * 2**20)


def join(limits, packed, halves, spots, rows):
    cache_len, width = halves[0].shape
    shape = (cache_len + len(spots) * (KVH + 1) * rows, 2 * width)
    return pl.pallas_call(
        functools.partial(join_kernel, spots, rows),
        out_shape=jax.ShapeDtypeStruct(shape, packed.dtype),
        in_specs=[VMEM] * 4,
        out_specs=VMEM,
        compiler_params=PARAMS,
        cost_estimate=pl.CostEstimate(flops=0, bytes_accessed=4 * shape[0] * shape[1], transcendentals=0),
        name="join",
    )(limits, packed, *halves)


def attend_step(limits, packed, spots, blocks, rows, cache_len):
    kinds = tuple(kind for kind, _ in blocks)
    arrays = [a for _, arrays in blocks for a in arrays]
    return pl.pallas_call(
        functools.partial(step_kernel, spots, kinds, rows, cache_len),
        out_shape=jax.ShapeDtypeStruct((len(spots) * rows, packed.shape[1]), packed.dtype),
        in_specs=[VMEM] * (2 + len(arrays)),
        out_specs=VMEM,
        compiler_params=PARAMS,
        cost_estimate=cost(spots, rows, cache_len),
        name="attend_%d" % spots[0],
    )(limits, packed, *arrays)


def attend_guests(guests, block, rows, cache_len):
    width = QH * HD
    return pl.pallas_call(
        functools.partial(guest_kernel, len(guests), rows, cache_len),
        out_shape=[jax.ShapeDtypeStruct((rows, width), g.dtype) for g in guests],
        in_specs=[VMEM] * (1 + len(guests)),
        out_specs=[VMEM] * len(guests),
        compiler_params=PARAMS,
        cost_estimate=cost(guests, rows, cache_len),
        name="attend_guests",
    )(block, *guests)


def place_rows(where, held, held_spots, rows, out, shape):
    again = out is not None
    return pl.pallas_call(
        functools.partial(place_kernel, tuple(held_spots), rows, again),
        out_shape=jax.ShapeDtypeStruct(shape, held[0].dtype),
        in_specs=[SMEM] + [ANY] * (again + len(held)),
        out_specs=ANY,
        scratch_shapes=[pltpu.SemaphoreType.DMA((sum(len(s) for s in held_spots),))],
        input_output_aliases={1: 0} if again else {},
        compiler_params=PARAMS,
        cost_estimate=pl.CostEstimate(flops=0, bytes_accessed=2 * held[0].size, transcendentals=0),
        name="place_last" if again else "place_held",
    )(where, *([out] if again else []), *held)


def move_rows(targets, rows):
    count = rows.shape[0]
    pick = (jnp.arange(count, dtype=jnp.int32)[:, None] == targets[None, :]).astype(rows.dtype)
    return jnp.dot(pick, rows, preferred_element_type=jnp.float32).astype(rows.dtype)


def tie(values, after):
    return lax.optimization_barrier((values, after))


def body(queries, send_list, recv_list, slot_pos, pack_seq, seq_kv):
    query_rows = queries[0, 0]
    row_count, width = query_rows.shape
    dp_count = lax.axis_size("dp")
    ring = lax.axis_size("prompt")
    group_rows = row_count // ring
    me = lax.axis_index("prompt")
    kv = seq_kv[0, 0]

    def shifted(x, by):
        return lax.ppermute(x, "prompt", [(i, (i + by) % ring) for i in range(ring)])

    steps = ring // 2

    ordered = move_rows(send_list[0, 0], query_rows)
    arrived = lax.all_to_all(
        ordered.reshape(dp_count, row_count // dp_count, width), "dp", split_axis=0, concat_axis=0, tiled=True
    ).reshape(row_count, width)

    sequences = pack_seq[0, 0]
    behind = (me - sequences) % ring
    place = jnp.where(
        behind == 0,
        ring - 1,
        jnp.where(behind <= steps, 2 * (behind - 1), 2 * (ring - behind - 1) + 1),
    )
    spots = jnp.arange(ring, dtype=jnp.int32)
    at_place = place[None, :] == spots[:, None]
    where = jnp.sum(jnp.where(at_place, spots[None, :], 0), axis=1)
    grouped_pos = slot_pos[0, 0].reshape(ring, group_rows)
    limits = jnp.sum(jnp.where(at_place[:, :, None], grouped_pos[None], 0), axis=1)
    limits = jnp.tile(limits, (1, GROUPS))
    slot = recv_list[0, 0]
    of_group = (slot // group_rows)[:, None] == spots[None, :]
    target = jnp.sum(jnp.where(of_group, place[None, :], 0), axis=1) * group_rows + slot % group_rows
    packed = move_rows(target, arrived)

    far = steps - 2
    cache_len = kv.shape[0]
    mine, behind_far, ahead_far, opposite = (ring - 1,), (2 * far,), (2 * far + 1,), (2 * far + 2,)
    guest_rows = (KVH + 1) * group_rows

    span, half = KVH * HD, HALF * HD

    def halves_of(block):
        return tuple(
            jnp.concatenate([block[:, lo : lo + half], block[:, span + lo : span + lo + half]], axis=1)
            for lo in (0, half)
        )

    held, held_spots = [], []

    def score(spot_list, blocks):
        held.append(attend_step(limits, packed, spot_list, blocks, group_rows, cache_len))
        held_spots.append(spot_list)

    up, down = shifted(kv, 1), shifted(kv, -1)
    blocks_of = [[("cached", [up]), ("cached", [down])]]
    up, down = halves_of(up), halves_of(down)
    for step in (1, 2):
        if step == 2:
            first, ordered = tie(up[0], ordered)
            up = (first, up[1])
        up = tuple(shifted(x, 1) for x in up)
        down = tuple(shifted(x, -1) for x in down)
        blocks_of.append([("halves", list(up)), ("halves", list(down))])
    up = join(limits, packed, up, ahead_far, group_rows)
    down = join(limits, packed, down, opposite + behind_far, group_rows)
    up, down = shifted(up, 1), shifted(down, -1)
    blocks_of.append([("joined", [up]), ("joined", [down])])
    ahead_guest, behind_guest = up[cache_len:], down[cache_len + guest_rows :]
    score(mine, [("cached", [kv])])
    score((0, 1), blocks_of[0])
    score((2, 3), blocks_of[1])
    up, held = tie(up[:cache_len], held)
    up, down = shifted(up, 1), shifted(down[: cache_len + guest_rows], -1)
    blocks_of.append([("joined", [up]), ("joined", [down])])
    opposite_guest = down[cache_len:]
    score((4, 5), blocks_of[2])
    up, held = tie(up, held)
    up, down = shifted(up, 1), shifted(down[:cache_len], -1)
    score((6, 7), blocks_of[3])
    score((8, 9), blocks_of[4])
    out = place_rows(where, held, held_spots, group_rows, None, packed.shape)
    up, out = tie(up, out)
    opposite_out, behind_out = attend_guests([opposite_guest, behind_guest], up, group_rows, cache_len)
    opposite_out, behind_out = shifted(opposite_out, 2), shifted(behind_out, 1)
    (ahead_out,) = attend_guests([ahead_guest], down, group_rows, cache_len)
    ahead_out = shifted(ahead_out, -1)
    held, held_spots = [], []
    score((2 * far - 2, 2 * far - 1), [("joined", [up]), ("joined", [down])])
    out = place_rows(
        where,
        [*held, opposite_out, behind_out, ahead_out],
        [*held_spots, opposite, behind_far, ahead_far],
        group_rows,
        out,
        packed.shape,
    )
    return out[None, None]


def solution(mesh):
    return jax.shard_map(
        body,
        mesh=mesh,
        in_specs=(
            P("prompt", "dp", None, None),
            P("prompt", "dp", None),
            P("prompt", "dp", None),
            P("prompt", "dp", None),
            P("prompt", "dp", None),
            P("dp", "prompt", None, None),
        ),
        out_specs=P("prompt", "dp", None, None),
        check_vma=False,
    )
```

```python
import functools
import math

import jax
import jax.numpy as jnp
from jax import lax
from jax.experimental import pallas as pl
from jax.experimental.pallas import tpu as pltpu
from jax.sharding import PartitionSpec as P

HD = 128
QH = 32
KVH = 4
GROUPS = QH // KVH
SCALE = math.log2(math.e) / math.sqrt(HD)


def score_group(query_ref, row, rows, block, limits, out_ref, out_row):
    cache_len = block.shape[0]
    visible = lax.broadcasted_iota(jnp.int32, (cache_len, GROUPS * rows), 0) <= limits
    for k in range(KVH):
        heads = [slice((k * GROUPS + g) * HD, (k * GROUPS + g + 1) * HD) for g in range(GROUPS)]
        query = jnp.concatenate([query_ref[row : row + rows, h] for h in heads], axis=0)
        scores = lax.dot_general(
            block[:, k * HD : (k + 1) * HD],
            query,
            (((1,), (1,)), ((), ())),
            preferred_element_type=jnp.float32,
        )
        scores = jnp.where(visible, scores, -jnp.inf)
        row_max = jnp.max(scores, axis=0, keepdims=True)
        exponent = jnp.exp2((scores - row_max) * SCALE)
        row_total = jnp.sum(exponent, axis=0, keepdims=True)
        mixed = lax.dot_general(
            exponent.astype(jnp.bfloat16),
            block[:, (KVH + k) * HD : (KVH + k + 1) * HD],
            (((0,), (0,)), ((), ())),
            preferred_element_type=jnp.float32,
        )
        mixed = (mixed / row_total.reshape(GROUPS * rows, 1)).astype(jnp.bfloat16)
        for g in range(GROUPS):
            out_ref[out_row : out_row + rows, heads[g]] = mixed[g * rows : (g + 1) * rows]


def step_kernel(spots, rows, limits_ref, query_ref, *refs):
    blocks, out_ref = refs[:-1], refs[-1]
    for i, spot in enumerate(spots):
        score_group(query_ref, spot * rows, rows, blocks[i], limits_ref[spot : spot + 1, :], out_ref, i * rows)


def guest_kernel(sources, rows, *refs):
    count = len(sources)
    blocks, guests, outs = refs[: -2 * count], refs[-2 * count : -count], refs[-count:]
    for source, guest_ref, out_ref in zip(sources, guests, outs):
        width = out_ref.shape[1]
        parts = guest_ref[:, width:].astype(jnp.float32)
        limits = (parts[0:1] * 16.0 + parts[1:2]).astype(jnp.int32)
        score_group(guest_ref, 0, rows, blocks[source], limits, out_ref, 0)


def place_kernel(ref_spots, rows, again, where_ref, *refs):
    if again:
        refs = refs[1:]
    held, out_ref, sems = refs[: len(ref_spots)], refs[-2], refs[-1]
    copies = []
    for ref, spots in zip(held, ref_spots):
        for i, spot in enumerate(spots):
            start = pl.multiple_of(where_ref[spot] * rows, rows)
            copy = pltpu.make_async_copy(
                ref.at[pl.ds(i * rows, rows), :], out_ref.at[pl.ds(start, rows), :], sems.at[len(copies)]
            )
            copy.start()
            copies.append(copy)
    for copy in copies:
        copy.wait()


def cost(spots, rows, cache_len):
    work = len(spots) * rows * QH * cache_len
    return pl.CostEstimate(flops=4 * work * HD, bytes_accessed=2**20, transcendentals=work)


VMEM = pl.BlockSpec(memory_space=pltpu.VMEM)
SMEM = pl.BlockSpec(memory_space=pltpu.SMEM)
ANY = pl.BlockSpec(memory_space=pl.ANY)
PARAMS = pltpu.CompilerParams(vmem_limit_bytes=10 * 2**20)


def attend_step(limits, packed, spots, blocks, rows):
    return pl.pallas_call(
        functools.partial(step_kernel, spots, rows),
        out_shape=jax.ShapeDtypeStruct((len(spots) * rows, packed.shape[1]), packed.dtype),
        in_specs=[VMEM] * (2 + len(spots)),
        out_specs=VMEM,
        compiler_params=PARAMS,
        cost_estimate=cost(spots, rows, blocks[0].shape[0]),
        name="attend_%d" % spots[0],
    )(limits, packed, *blocks)


def attend_guests(guests, sources, blocks, rows):
    width = guests[0].shape[1] - HD
    return pl.pallas_call(
        functools.partial(guest_kernel, sources, rows),
        out_shape=[jax.ShapeDtypeStruct((rows, width), g.dtype) for g in guests],
        in_specs=[VMEM] * (len(blocks) + len(guests)),
        out_specs=[VMEM] * len(guests),
        compiler_params=PARAMS,
        cost_estimate=cost(guests, rows, blocks[0].shape[0]),
        name="attend_guests",
    )(*blocks, *guests)


def place_rows(where, held, held_spots, rows, out, shape):
    again = out is not None
    return pl.pallas_call(
        functools.partial(place_kernel, tuple(held_spots), rows, again),
        out_shape=jax.ShapeDtypeStruct(shape, held[0].dtype),
        in_specs=[SMEM] + [ANY] * (again + len(held)),
        out_specs=ANY,
        scratch_shapes=[pltpu.SemaphoreType.DMA((sum(len(s) for s in held_spots),))],
        input_output_aliases={1: 0} if again else {},
        compiler_params=PARAMS,
        cost_estimate=pl.CostEstimate(flops=0, bytes_accessed=2 * held[0].size, transcendentals=0),
        name="place_last" if again else "place_held",
    )(where, *([out] if again else []), *held)


def move_rows(targets, rows):
    count = rows.shape[0]
    pick = (jnp.arange(count, dtype=jnp.int32)[:, None] == targets[None, :]).astype(rows.dtype)
    return jnp.dot(pick, rows, preferred_element_type=jnp.float32).astype(rows.dtype)


def tie(values, after):
    return lax.optimization_barrier((values, after))


def body(queries, send_list, recv_list, slot_pos, pack_seq, seq_kv):
    query_rows = queries[0, 0]
    row_count, width = query_rows.shape
    dp_count = lax.axis_size("dp")
    ring = lax.axis_size("prompt")
    group_rows = row_count // ring
    me = lax.axis_index("prompt")
    kv = seq_kv[0, 0]

    turn = 1 - 2 * (lax.axis_index("dp") % 2)

    def shifted(x, by):
        pairs = [
            (d * ring + i, d * ring + (i + by * (1 - 2 * (d % 2))) % ring) for d in range(dp_count) for i in range(ring)
        ]
        return lax.ppermute(x, ("dp", "prompt"), pairs)

    steps = ring // 2

    ordered = move_rows(send_list[0, 0], query_rows)
    arrived = lax.all_to_all(
        ordered.reshape(dp_count, row_count // dp_count, width), "dp", split_axis=0, concat_axis=0, tiled=True
    ).reshape(row_count, width)

    sequences = pack_seq[0, 0]
    behind = (turn * (me - sequences)) % ring
    place = jnp.where(
        behind == 0,
        ring - 1,
        jnp.where(behind <= steps, 2 * (behind - 1), 2 * (ring - behind - 1) + 1),
    )
    spots = jnp.arange(ring, dtype=jnp.int32)
    at_place = place[None, :] == spots[:, None]
    where = jnp.sum(jnp.where(at_place, spots[None, :], 0), axis=1)
    grouped_pos = slot_pos[0, 0].reshape(ring, group_rows)
    limits = jnp.sum(jnp.where(at_place[:, :, None], grouped_pos[None], 0), axis=1)
    limits = jnp.tile(limits, (1, GROUPS))
    slot = recv_list[0, 0]
    of_group = (slot // group_rows)[:, None] == spots[None, :]
    target = jnp.sum(jnp.where(of_group, place[None, :], 0), axis=1) * group_rows + slot % group_rows
    packed = move_rows(target, arrived)

    far = steps - 2
    mine, behind_far, ahead_far, opposite = (ring - 1,), (2 * far,), (2 * far + 1,), (2 * far + 2,)

    def payload(spot):
        rows = packed[spot * group_rows : (spot + 1) * group_rows]
        parts = jnp.stack([limits[spot] // 16, limits[spot] % 16]).astype(rows.dtype)
        beside = jnp.pad(parts, ((0, group_rows - 2), (0, 0)))
        return jnp.concatenate([rows, beside], axis=1)

    up, down = kv, kv
    held, held_spots = [], []
    blocks_of = []

    def score(spot_list, blocks):
        held.append(attend_step(limits, packed, spot_list, blocks, group_rows))
        held_spots.append(spot_list)

    for step in range(far):
        if step == 2:
            up, ordered = tie(up, ordered)
        if step == 3:
            guests = [payload(s[0]) for s in (opposite, behind_far, ahead_far)]
            up, guests = tie(up, guests)
            guests[0] = shifted(guests[0], -2)
        if step == 4:
            score(mine, (kv,))
            score((0, 1), blocks_of[0])
            up, (guests, held) = tie(up, (guests, held))
            guests[1], guests[2] = shifted(guests[1], -1), shifted(guests[2], 1)
        if step == 5:
            score((2, 3), blocks_of[1])
            score((4, 5), blocks_of[2])
            up, (guests, held) = tie(up, (guests, held))
        up = shifted(up, 1)
        down = shifted(down, -1)
        blocks_of.append((up, down))
    score((6, 7), blocks_of[3])
    score((8, 9), blocks_of[4])
    out = place_rows(where, held, held_spots, group_rows, None, packed.shape)
    up, out = tie(up, out)
    back = attend_guests(guests, (0, 0, 1), (up, down), group_rows)
    back = [shifted(g, by) for g, by in zip(back, (2, 1, -1))]
    held, held_spots = [], []
    score((2 * far - 2, 2 * far - 1), (up, down))
    out = place_rows(
        where, [*held, *back], [*held_spots, opposite, behind_far, ahead_far], group_rows, out, packed.shape
    )
    return out[None, None]


def solution(mesh):
    return jax.shard_map(
        body,
        mesh=mesh,
        in_specs=(
            P("prompt", "dp", None, None),
            P("prompt", "dp", None),
            P("prompt", "dp", None),
            P("prompt", "dp", None),
            P("prompt", "dp", None),
            P("dp", "prompt", None, None),
        ),
        out_specs=P("prompt", "dp", None, None),
        check_vma=False,
    )
```

```python
import functools
import math

import jax
import jax.numpy as jnp
from jax import lax
from jax.experimental import pallas as pl
from jax.experimental.pallas import tpu as pltpu
from jax.sharding import PartitionSpec as P

HD = 128
QH = 32
KVH = 4
GROUPS = QH // KVH
SCALE = math.log2(math.e) / math.sqrt(HD)


def score_group(query_of, rows, block, cache_len, limits, out_ref, out_row):
    visible = lax.broadcasted_iota(jnp.int32, (cache_len, GROUPS * rows), 0) <= limits
    for k in range(KVH):
        key_at, value_at = k * HD, (KVH + k) * HD
        query = jnp.concatenate([query_of(k, g) for g in range(GROUPS)], axis=0)
        scores = lax.dot_general(
            block[:cache_len, key_at : key_at + HD],
            query,
            (((1,), (1,)), ((), ())),
            preferred_element_type=jnp.float32,
        )
        scores = jnp.where(visible, scores, -jnp.inf)
        row_max = jnp.max(scores, axis=0, keepdims=True)
        exponent = jnp.exp2((scores - row_max) * SCALE)
        row_total = jnp.sum(exponent, axis=0, keepdims=True)
        mixed = lax.dot_general(
            exponent.astype(jnp.bfloat16),
            block[:cache_len, value_at : value_at + HD],
            (((0,), (0,)), ((), ())),
            preferred_element_type=jnp.float32,
        )
        mixed = (mixed / row_total.reshape(GROUPS * rows, 1)).astype(jnp.bfloat16)
        for g in range(GROUPS):
            column = (k * GROUPS + g) * HD
            out_ref[out_row : out_row + rows, column : column + HD] = mixed[g * rows : (g + 1) * rows]


def step_kernel(spots, rows, cache_len, limits_ref, query_ref, *refs):
    blocks, out_ref = refs[:-1], refs[-1]
    for i, spot in enumerate(spots):

        def query_of(k, g, row=spot * rows):
            return query_ref[row : row + rows, (k * GROUPS + g) * HD : (k * GROUPS + g + 1) * HD]

        score_group(query_of, rows, blocks[i], cache_len, limits_ref[spot : spot + 1, :], out_ref, i * rows)


def guest_kernel(count, rows, cache_len, block, *refs):
    for guest_ref, out_ref in zip(refs[:count], refs[count:]):
        places = guest_ref[KVH * rows : (KVH + 1) * rows, :HD].astype(jnp.float32)
        limits = (places[0:1] * 16.0 + places[1:2]).astype(jnp.int32)

        def query_of(k, g, guest_ref=guest_ref):
            return guest_ref[k * rows : (k + 1) * rows, g * HD : (g + 1) * HD]

        score_group(query_of, rows, block, cache_len, limits, out_ref, 0)


def place_kernel(ref_spots, rows, again, where_ref, *refs):
    if again:
        refs = refs[1:]
    held, out_ref, sems = refs[: len(ref_spots)], refs[-2], refs[-1]
    copies = []
    for ref, spots in zip(held, ref_spots):
        for i, spot in enumerate(spots):
            start = pl.multiple_of(where_ref[spot] * rows, rows)
            copy = pltpu.make_async_copy(
                ref.at[pl.ds(i * rows, rows), :], out_ref.at[pl.ds(start, rows), :], sems.at[len(copies)]
            )
            copy.start()
            copies.append(copy)
    for copy in copies:
        copy.wait()


def join_kernel(spots, rows, limits_ref, query_ref, block_ref, out_ref):
    cache_len, width = block_ref.shape
    out_ref[:cache_len, :] = block_ref[...]
    for i, spot in enumerate(spots):
        base = cache_len + i * (KVH + 1) * rows
        for k in range(KVH):
            heads = query_ref[spot * rows : (spot + 1) * rows, k * width : (k + 1) * width]
            out_ref[base + k * rows : base + (k + 1) * rows, :] = heads
        places = jnp.broadcast_to(limits_ref[spot : spot + 1, :], (rows, limits_ref.shape[1]))
        row = lax.broadcasted_iota(jnp.int32, places.shape, 0)
        places = jnp.where(row == 0, places >> 4, jnp.where(row == 1, places & 15, 0))
        below = base + KVH * rows
        out_ref[below : below + rows, :] = jnp.zeros((rows, width), out_ref.dtype)
        out_ref[below : below + rows, : places.shape[1]] = places.astype(jnp.float32).astype(out_ref.dtype)


def cost(spots, rows, cache_len):
    work = len(spots) * rows * QH * cache_len
    return pl.CostEstimate(flops=4 * work * HD, bytes_accessed=2**20, transcendentals=work)


VMEM = pl.BlockSpec(memory_space=pltpu.VMEM)
SMEM = pl.BlockSpec(memory_space=pltpu.SMEM)
ANY = pl.BlockSpec(memory_space=pl.ANY)
PARAMS = pltpu.CompilerParams(vmem_limit_bytes=10 * 2**20)


def join(limits, packed, block, spots, rows):
    cache_len, width = block.shape
    shape = (cache_len + len(spots) * (KVH + 1) * rows, width)
    return pl.pallas_call(
        functools.partial(join_kernel, spots, rows),
        out_shape=jax.ShapeDtypeStruct(shape, packed.dtype),
        in_specs=[VMEM] * 3,
        out_specs=VMEM,
        compiler_params=PARAMS,
        cost_estimate=pl.CostEstimate(flops=0, bytes_accessed=4 * shape[0] * shape[1], transcendentals=0),
        name="join",
    )(limits, packed, block)


def attend_step(limits, packed, spots, blocks, rows, cache_len):
    return pl.pallas_call(
        functools.partial(step_kernel, spots, rows, cache_len),
        out_shape=jax.ShapeDtypeStruct((len(spots) * rows, packed.shape[1]), packed.dtype),
        in_specs=[VMEM] * (2 + len(blocks)),
        out_specs=VMEM,
        compiler_params=PARAMS,
        cost_estimate=cost(spots, rows, cache_len),
        name="attend_%d" % spots[0],
    )(limits, packed, *blocks)


def attend_guests(guests, block, rows, cache_len):
    width = QH * HD
    return pl.pallas_call(
        functools.partial(guest_kernel, len(guests), rows, cache_len),
        out_shape=[jax.ShapeDtypeStruct((rows, width), g.dtype) for g in guests],
        in_specs=[VMEM] * (1 + len(guests)),
        out_specs=[VMEM] * len(guests),
        compiler_params=PARAMS,
        cost_estimate=cost(guests, rows, cache_len),
        name="attend_guests",
    )(block, *guests)


def place_rows(where, held, held_spots, rows, out, shape):
    again = out is not None
    return pl.pallas_call(
        functools.partial(place_kernel, tuple(held_spots), rows, again),
        out_shape=jax.ShapeDtypeStruct(shape, held[0].dtype),
        in_specs=[SMEM] + [ANY] * (again + len(held)),
        out_specs=ANY,
        scratch_shapes=[pltpu.SemaphoreType.DMA((sum(len(s) for s in held_spots),))],
        input_output_aliases={1: 0} if again else {},
        compiler_params=PARAMS,
        cost_estimate=pl.CostEstimate(flops=0, bytes_accessed=2 * held[0].size, transcendentals=0),
        name="place_last" if again else "place_held",
    )(where, *([out] if again else []), *held)


def move_rows(targets, rows):
    count = rows.shape[0]
    pick = (jnp.arange(count, dtype=jnp.int32)[:, None] == targets[None, :]).astype(rows.dtype)
    return jnp.dot(pick, rows, preferred_element_type=jnp.float32).astype(rows.dtype)


def tie(values, after):
    return lax.optimization_barrier((values, after))


def body(queries, send_list, recv_list, slot_pos, pack_seq, seq_kv):
    query_rows = queries[0, 0]
    row_count, width = query_rows.shape
    dp_count = lax.axis_size("dp")
    ring = lax.axis_size("prompt")
    group_rows = row_count // ring
    me = lax.axis_index("prompt")
    kv = seq_kv[0, 0]

    def shifted(x, by):
        return lax.ppermute(x, "prompt", [(i, (i + by) % ring) for i in range(ring)])

    steps = ring // 2

    ordered = move_rows(send_list[0, 0], query_rows)
    arrived = lax.all_to_all(
        ordered.reshape(dp_count, row_count // dp_count, width), "dp", split_axis=0, concat_axis=0, tiled=True
    ).reshape(row_count, width)

    sequences = pack_seq[0, 0]
    behind = (me - sequences) % ring
    place = jnp.where(
        behind == 0,
        ring - 1,
        jnp.where(behind <= steps, 2 * (behind - 1), 2 * (ring - behind - 1) + 1),
    )
    spots = jnp.arange(ring, dtype=jnp.int32)
    at_place = place[None, :] == spots[:, None]
    where = jnp.sum(jnp.where(at_place, spots[None, :], 0), axis=1)
    grouped_pos = slot_pos[0, 0].reshape(ring, group_rows)
    limits = jnp.sum(jnp.where(at_place[:, :, None], grouped_pos[None], 0), axis=1)
    limits = jnp.tile(limits, (1, GROUPS))
    slot = recv_list[0, 0]
    of_group = (slot // group_rows)[:, None] == spots[None, :]
    target = jnp.sum(jnp.where(of_group, place[None, :], 0), axis=1) * group_rows + slot % group_rows
    packed = move_rows(target, arrived)

    far = steps - 2
    cache_len = kv.shape[0]
    mine, behind_far, ahead_far, opposite = (ring - 1,), (2 * far,), (2 * far + 1,), (2 * far + 2,)
    guest_rows = (KVH + 1) * group_rows

    held, held_spots = [], []

    def score(spot_list, blocks):
        held.append(attend_step(limits, packed, spot_list, blocks, group_rows, cache_len))
        held_spots.append(spot_list)

    def turn(up, down, down_rows=None):
        down, _ = tie(down, up if up is not kv else place)
        return shifted(up, 1), shifted(down[:down_rows], -1)

    up, down = kv, kv
    blocks_of = []
    for step in range(3):
        if step == 1:
            up, ordered = tie(up, ordered)
        if step == 2:
            up, arrived = tie(up, arrived)
        up, down = turn(up, down)
        blocks_of.append((up, down))
    up = join(limits, packed, up, ahead_far, group_rows)
    down = join(limits, packed, down, opposite + behind_far, group_rows)
    up, down = turn(up, down)
    blocks_of.append((up, down))
    ahead_guest, behind_guest = up[cache_len:], down[cache_len + guest_rows :]
    score(mine, (kv,))
    score((0, 1), blocks_of[0])
    up, held = tie(up[:cache_len], held)
    up, down = turn(up, down, cache_len + guest_rows)
    blocks_of.append((up, down))
    opposite_guest = down[cache_len:]
    score((2, 3), blocks_of[1])
    score((4, 5), blocks_of[2])
    up, held = tie(up, held)
    up, down = turn(up, down, cache_len)
    score((6, 7), blocks_of[3])
    score((8, 9), blocks_of[4])
    out = place_rows(where, held, held_spots, group_rows, None, packed.shape)
    up, out = tie(up, out)
    opposite_out, behind_out = attend_guests([opposite_guest, behind_guest], up, group_rows, cache_len)
    opposite_out, behind_out = shifted(opposite_out, 2), shifted(behind_out, 1)
    (ahead_out,) = attend_guests([ahead_guest], down, group_rows, cache_len)
    ahead_out = shifted(ahead_out, -1)
    held, held_spots = [], []
    score((2 * far - 2, 2 * far - 1), (up, down))
    out = place_rows(
        where,
        [*held, opposite_out, behind_out, ahead_out],
        [*held_spots, opposite, behind_far, ahead_far],
        group_rows,
        out,
        packed.shape,
    )
    return out[None, None]


def solution(mesh):
    return jax.shard_map(
        body,
        mesh=mesh,
        in_specs=(
            P("prompt", "dp", None, None),
            P("prompt", "dp", None),
            P("prompt", "dp", None),
            P("prompt", "dp", None),
            P("prompt", "dp", None),
            P("dp", "prompt", None, None),
        ),
        out_specs=P("prompt", "dp", None, None),
        check_vma=False,
    )
```

```python
import functools
import math

import jax
import jax.numpy as jnp
from jax import lax
from jax.experimental import pallas as pl
from jax.experimental.pallas import tpu as pltpu
from jax.sharding import PartitionSpec as P

HD = 128
QH = 32
KVH = 4
GROUPS = QH // KVH
SCALE = math.log2(math.e) / math.sqrt(HD)


def score_group(query_ref, row, rows, block, limits, out_ref, out_row):
    cache_len = block.shape[0]
    visible = lax.broadcasted_iota(jnp.int32, (cache_len, GROUPS * rows), 0) <= limits
    for k in range(KVH):
        heads = [slice((k * GROUPS + g) * HD, (k * GROUPS + g + 1) * HD) for g in range(GROUPS)]
        query = jnp.concatenate([query_ref[row : row + rows, h] for h in heads], axis=0)
        scores = lax.dot_general(
            block[:, k * HD : (k + 1) * HD],
            query,
            (((1,), (1,)), ((), ())),
            preferred_element_type=jnp.float32,
        )
        scores = jnp.where(visible, scores, -jnp.inf)
        row_max = jnp.max(scores, axis=0, keepdims=True)
        exponent = jnp.exp2((scores - row_max) * SCALE)
        row_total = jnp.sum(exponent, axis=0, keepdims=True)
        mixed = lax.dot_general(
            exponent.astype(jnp.bfloat16),
            block[:, (KVH + k) * HD : (KVH + k + 1) * HD],
            (((0,), (0,)), ((), ())),
            preferred_element_type=jnp.float32,
        )
        mixed = (mixed / row_total.reshape(GROUPS * rows, 1)).astype(jnp.bfloat16)
        for g in range(GROUPS):
            out_ref[out_row : out_row + rows, heads[g]] = mixed[g * rows : (g + 1) * rows]


def step_kernel(spots, rows, limits_ref, query_ref, *refs):
    blocks, out_ref = refs[:-1], refs[-1]
    for i, spot in enumerate(spots):
        score_group(query_ref, spot * rows, rows, blocks[i], limits_ref[spot : spot + 1, :], out_ref, i * rows)


def guest_kernel(sources, rows, *refs):
    count = len(sources)
    blocks, guests, outs = refs[: -2 * count], refs[-2 * count : -count], refs[-count:]
    for source, guest_ref, out_ref in zip(sources, guests, outs):
        width = out_ref.shape[1]
        parts = guest_ref[:, width:].astype(jnp.float32)
        limits = (parts[0:1] * 16.0 + parts[1:2]).astype(jnp.int32)
        score_group(guest_ref, 0, rows, blocks[source], limits, out_ref, 0)


def place_kernel(ref_spots, rows, again, where_ref, *refs):
    if again:
        refs = refs[1:]
    held, out_ref, sems = refs[: len(ref_spots)], refs[-2], refs[-1]
    copies = []
    for ref, spots in zip(held, ref_spots):
        for i, spot in enumerate(spots):
            start = pl.multiple_of(where_ref[spot] * rows, rows)
            copy = pltpu.make_async_copy(
                ref.at[pl.ds(i * rows, rows), :], out_ref.at[pl.ds(start, rows), :], sems.at[len(copies)]
            )
            copy.start()
            copies.append(copy)
    for copy in copies:
        copy.wait()


def cost(spots, rows, cache_len):
    work = len(spots) * rows * QH * cache_len
    return pl.CostEstimate(flops=4 * work * HD, bytes_accessed=2**20, transcendentals=work)


VMEM = pl.BlockSpec(memory_space=pltpu.VMEM)
SMEM = pl.BlockSpec(memory_space=pltpu.SMEM)
ANY = pl.BlockSpec(memory_space=pl.ANY)
PARAMS = pltpu.CompilerParams(vmem_limit_bytes=10 * 2**20)


def attend_step(limits, packed, spots, blocks, rows):
    return pl.pallas_call(
        functools.partial(step_kernel, spots, rows),
        out_shape=jax.ShapeDtypeStruct((len(spots) * rows, packed.shape[1]), packed.dtype),
        in_specs=[VMEM] * (2 + len(spots)),
        out_specs=VMEM,
        compiler_params=PARAMS,
        cost_estimate=cost(spots, rows, blocks[0].shape[0]),
        name="attend_%d" % spots[0],
    )(limits, packed, *blocks)


def attend_guests(guests, sources, blocks, rows):
    width = guests[0].shape[1] - HD
    return pl.pallas_call(
        functools.partial(guest_kernel, sources, rows),
        out_shape=[jax.ShapeDtypeStruct((rows, width), g.dtype) for g in guests],
        in_specs=[VMEM] * (len(blocks) + len(guests)),
        out_specs=[VMEM] * len(guests),
        compiler_params=PARAMS,
        cost_estimate=cost(guests, rows, blocks[0].shape[0]),
        name="attend_guests",
    )(*blocks, *guests)


def place_rows(where, held, held_spots, rows, out, shape):
    again = out is not None
    return pl.pallas_call(
        functools.partial(place_kernel, tuple(held_spots), rows, again),
        out_shape=jax.ShapeDtypeStruct(shape, held[0].dtype),
        in_specs=[SMEM] + [ANY] * (again + len(held)),
        out_specs=ANY,
        scratch_shapes=[pltpu.SemaphoreType.DMA((sum(len(s) for s in held_spots),))],
        input_output_aliases={1: 0} if again else {},
        compiler_params=PARAMS,
        cost_estimate=pl.CostEstimate(flops=0, bytes_accessed=2 * held[0].size, transcendentals=0),
        name="place_last" if again else "place_held",
    )(where, *([out] if again else []), *held)


def move_rows(targets, rows):
    count = rows.shape[0]
    pick = (jnp.arange(count, dtype=jnp.int32)[:, None] == targets[None, :]).astype(rows.dtype)
    return jnp.dot(pick, rows, preferred_element_type=jnp.float32).astype(rows.dtype)


def tie(values, after):
    return lax.optimization_barrier((values, after))


def body(queries, send_list, recv_list, slot_pos, pack_seq, seq_kv):
    query_rows = queries[0, 0]
    row_count, width = query_rows.shape
    dp_count = lax.axis_size("dp")
    ring = lax.axis_size("prompt")
    group_rows = row_count // ring
    me = lax.axis_index("prompt")
    kv = seq_kv[0, 0]

    def shifted(x, by):
        return lax.ppermute(x, "prompt", [(i, (i + by) % ring) for i in range(ring)])

    steps = ring // 2

    ordered = move_rows(send_list[0, 0], query_rows)
    arrived = lax.all_to_all(
        ordered.reshape(dp_count, row_count // dp_count, width), "dp", split_axis=0, concat_axis=0, tiled=True
    ).reshape(row_count, width)

    sequences = pack_seq[0, 0]
    behind = (me - sequences) % ring
    place = jnp.where(
        behind == 0,
        ring - 1,
        jnp.where(behind <= steps, 2 * (behind - 1), 2 * (ring - behind - 1) + 1),
    )
    spots = jnp.arange(ring, dtype=jnp.int32)
    at_place = place[None, :] == spots[:, None]
    where = jnp.sum(jnp.where(at_place, spots[None, :], 0), axis=1)
    grouped_pos = slot_pos[0, 0].reshape(ring, group_rows)
    limits = jnp.sum(jnp.where(at_place[:, :, None], grouped_pos[None], 0), axis=1)
    limits = jnp.tile(limits, (1, GROUPS))
    slot = recv_list[0, 0]
    of_group = (slot // group_rows)[:, None] == spots[None, :]
    target = jnp.sum(jnp.where(of_group, place[None, :], 0), axis=1) * group_rows + slot % group_rows
    packed = move_rows(target, arrived)

    far = steps - 2
    mine, behind_far, ahead_far, opposite = (ring - 1,), (2 * far,), (2 * far + 1,), (2 * far + 2,)

    def payload(spot):
        rows = packed[spot * group_rows : (spot + 1) * group_rows]
        parts = jnp.stack([limits[spot] // 16, limits[spot] % 16]).astype(rows.dtype)
        beside = jnp.pad(parts, ((0, group_rows - 2), (0, 0)))
        return jnp.concatenate([rows, beside], axis=1)

    up, down = kv, kv
    held, held_spots = [], []
    blocks_of = []

    def score(spot_list, blocks):
        held.append(attend_step(limits, packed, spot_list, blocks, group_rows))
        held_spots.append(spot_list)

    for step in range(far):
        if step == 2:
            up, ordered = tie(up, ordered)
        if step == 3:
            guests = [payload(s[0]) for s in (opposite, behind_far, ahead_far)]
            guests[1], guests[2] = shifted(guests[1], -1), shifted(guests[2], 1)
            up, guests = tie(up, guests)
            guests[0] = shifted(guests[0], -2)
        if step == 4:
            score(mine, (kv,))
            score((0, 1), blocks_of[0])
            up, (guests, held) = tie(up, (guests, held))
        if step == 5:
            score((2, 3), blocks_of[1])
            score((4, 5), blocks_of[2])
            up, held = tie(up, held)
        up = shifted(up, 1)
        down = shifted(down, -1)
        blocks_of.append((up, down))
    score((6, 7), blocks_of[3])
    score((8, 9), blocks_of[4])
    out = place_rows(where, held, held_spots, group_rows, None, packed.shape)
    up, out = tie(up, out)
    back = attend_guests(guests[:2], (0, 0), (up,), group_rows)
    back = [shifted(g, by) for g, by in zip(back, (2, 1))]
    back += [shifted(g, -1) for g in attend_guests(guests[2:], (0,), (down,), group_rows)]
    held, held_spots = [], []
    score((2 * far - 2, 2 * far - 1), (up, down))
    out = place_rows(
        where, [*held, *back], [*held_spots, opposite, behind_far, ahead_far], group_rows, out, packed.shape
    )
    return out[None, None]


def solution(mesh):
    return jax.shard_map(
        body,
        mesh=mesh,
        in_specs=(
            P("prompt", "dp", None, None),
            P("prompt", "dp", None),
            P("prompt", "dp", None),
            P("prompt", "dp", None),
            P("prompt", "dp", None),
            P("dp", "prompt", None, None),
        ),
        out_specs=P("prompt", "dp", None, None),
        check_vma=False,
    )
```

```python
import functools
import math

import jax
import jax.numpy as jnp
from jax import lax
from jax.experimental import pallas as pl
from jax.experimental.pallas import tpu as pltpu
from jax.sharding import PartitionSpec as P

HD = 128
QH = 32
KVH = 4
GROUPS = QH // KVH
SCALE = math.log2(math.e) / math.sqrt(HD)


def score_group(query_ref, row, rows, block, limits, out_ref, out_row):
    cache_len = block.shape[0]
    visible = lax.broadcasted_iota(jnp.int32, (cache_len, GROUPS * rows), 0) <= limits
    for k in range(KVH):
        heads = [slice((k * GROUPS + g) * HD, (k * GROUPS + g + 1) * HD) for g in range(GROUPS)]
        query = jnp.concatenate([query_ref[row : row + rows, h] for h in heads], axis=0)
        scores = lax.dot_general(
            block[:, k * HD : (k + 1) * HD],
            query,
            (((1,), (1,)), ((), ())),
            preferred_element_type=jnp.float32,
        )
        scores = jnp.where(visible, scores, -jnp.inf)
        row_max = jnp.max(scores, axis=0, keepdims=True)
        exponent = jnp.exp2((scores - row_max) * SCALE)
        row_total = jnp.sum(exponent, axis=0, keepdims=True)
        mixed = lax.dot_general(
            exponent.astype(jnp.bfloat16),
            block[:, (KVH + k) * HD : (KVH + k + 1) * HD],
            (((0,), (0,)), ((), ())),
            preferred_element_type=jnp.float32,
        )
        mixed = (mixed / row_total.reshape(GROUPS * rows, 1)).astype(jnp.bfloat16)
        for g in range(GROUPS):
            out_ref[out_row : out_row + rows, heads[g]] = mixed[g * rows : (g + 1) * rows]


def step_kernel(spots, rows, limits_ref, query_ref, *refs):
    blocks, out_ref = refs[:-1], refs[-1]
    for i, spot in enumerate(spots):
        score_group(query_ref, spot * rows, rows, blocks[i], limits_ref[spot : spot + 1, :], out_ref, i * rows)


def guest_kernel(sources, rows, *refs):
    count = len(sources)
    blocks, guests, outs = refs[: -2 * count], refs[-2 * count : -count], refs[-count:]
    for source, guest_ref, out_ref in zip(sources, guests, outs):
        width = out_ref.shape[1]
        parts = guest_ref[:, width:].astype(jnp.float32)
        limits = (parts[0:1] * 16.0 + parts[1:2]).astype(jnp.int32)
        score_group(guest_ref, 0, rows, blocks[source], limits, out_ref, 0)


def place_kernel(ref_spots, rows, again, where_ref, *refs):
    if again:
        refs = refs[1:]
    held, out_ref, sems = refs[: len(ref_spots)], refs[-2], refs[-1]
    copies = []
    for ref, spots in zip(held, ref_spots):
        for i, spot in enumerate(spots):
            start = pl.multiple_of(where_ref[spot] * rows, rows)
            copy = pltpu.make_async_copy(
                ref.at[pl.ds(i * rows, rows), :], out_ref.at[pl.ds(start, rows), :], sems.at[len(copies)]
            )
            copy.start()
            copies.append(copy)
    for copy in copies:
        copy.wait()


def cost(spots, rows, cache_len):
    work = len(spots) * rows * QH * cache_len
    return pl.CostEstimate(flops=4 * work * HD, bytes_accessed=2**20, transcendentals=work)


VMEM = pl.BlockSpec(memory_space=pltpu.VMEM)
SMEM = pl.BlockSpec(memory_space=pltpu.SMEM)
ANY = pl.BlockSpec(memory_space=pl.ANY)
PARAMS = pltpu.CompilerParams(vmem_limit_bytes=10 * 2**20)


def attend_step(limits, packed, spots, blocks, rows):
    return pl.pallas_call(
        functools.partial(step_kernel, spots, rows),
        out_shape=jax.ShapeDtypeStruct((len(spots) * rows, packed.shape[1]), packed.dtype),
        in_specs=[VMEM] * (2 + len(spots)),
        out_specs=VMEM,
        compiler_params=PARAMS,
        cost_estimate=cost(spots, rows, blocks[0].shape[0]),
        name="attend_%d" % spots[0],
    )(limits, packed, *blocks)


def attend_guests(guests, sources, blocks, rows):
    width = guests[0].shape[1] - HD
    return pl.pallas_call(
        functools.partial(guest_kernel, sources, rows),
        out_shape=[jax.ShapeDtypeStruct((rows, width), g.dtype) for g in guests],
        in_specs=[VMEM] * (len(blocks) + len(guests)),
        out_specs=[VMEM] * len(guests),
        compiler_params=PARAMS,
        cost_estimate=cost(guests, rows, blocks[0].shape[0]),
        name="attend_guests",
    )(*blocks, *guests)


def place_rows(where, held, held_spots, rows, out, shape):
    again = out is not None
    return pl.pallas_call(
        functools.partial(place_kernel, tuple(held_spots), rows, again),
        out_shape=jax.ShapeDtypeStruct(shape, held[0].dtype),
        in_specs=[SMEM] + [ANY] * (again + len(held)),
        out_specs=ANY,
        scratch_shapes=[pltpu.SemaphoreType.DMA((sum(len(s) for s in held_spots),))],
        input_output_aliases={1: 0} if again else {},
        compiler_params=PARAMS,
        cost_estimate=pl.CostEstimate(flops=0, bytes_accessed=2 * held[0].size, transcendentals=0),
        name="place_last" if again else "place_held",
    )(where, *([out] if again else []), *held)


def move_rows(targets, rows):
    count = rows.shape[0]
    pick = (jnp.arange(count, dtype=jnp.int32)[:, None] == targets[None, :]).astype(rows.dtype)
    return jnp.dot(pick, rows, preferred_element_type=jnp.float32).astype(rows.dtype)


def tie(values, after):
    return lax.optimization_barrier((values, after))


def body(queries, send_list, recv_list, slot_pos, pack_seq, seq_kv):
    query_rows = queries[0, 0]
    row_count, width = query_rows.shape
    dp_count = lax.axis_size("dp")
    ring = lax.axis_size("prompt")
    group_rows = row_count // ring
    me = lax.axis_index("prompt")
    kv = seq_kv[0, 0]

    def shifted(x, by):
        return lax.ppermute(x, "prompt", [(i, (i + by) % ring) for i in range(ring)])

    steps = ring // 2

    ordered = move_rows(send_list[0, 0], query_rows)
    arrived = lax.all_to_all(
        ordered.reshape(dp_count, row_count // dp_count, width), "dp", split_axis=0, concat_axis=0, tiled=True
    ).reshape(row_count, width)

    sequences = pack_seq[0, 0]
    behind = (me - sequences) % ring
    place = jnp.where(
        behind == 0,
        ring - 1,
        jnp.where(behind <= steps, 2 * (behind - 1), 2 * (ring - behind - 1) + 1),
    )
    spots = jnp.arange(ring, dtype=jnp.int32)
    at_place = place[None, :] == spots[:, None]
    where = jnp.sum(jnp.where(at_place, spots[None, :], 0), axis=1)
    grouped_pos = slot_pos[0, 0].reshape(ring, group_rows)
    limits = jnp.sum(jnp.where(at_place[:, :, None], grouped_pos[None], 0), axis=1)
    limits = jnp.tile(limits, (1, GROUPS))
    slot = recv_list[0, 0]
    of_group = (slot // group_rows)[:, None] == spots[None, :]
    target = jnp.sum(jnp.where(of_group, place[None, :], 0), axis=1) * group_rows + slot % group_rows
    packed = move_rows(target, arrived)

    far = steps - 2
    mine, behind_far, ahead_far, opposite = (ring - 1,), (2 * far,), (2 * far + 1,), (2 * far + 2,)

    def payload(spot):
        rows = packed[spot * group_rows : (spot + 1) * group_rows]
        parts = jnp.stack([limits[spot] // 16, limits[spot] % 16]).astype(rows.dtype)
        beside = jnp.pad(parts, ((0, group_rows - 2), (0, 0)))
        return jnp.concatenate([rows, beside], axis=1)

    up, down = kv, kv
    held, held_spots = [], []
    blocks_of = []

    def score(spot_list, blocks):
        held.append(attend_step(limits, packed, spot_list, blocks, group_rows))
        held_spots.append(spot_list)

    for step in range(far):
        if step == 2:
            up, ordered = tie(up, ordered)
        if step == 3:
            guests = [payload(s[0]) for s in (opposite, behind_far, ahead_far)]
            up, guests = tie(up, guests)
            guests = [shifted(g, by) for g, by in zip(guests, (-2, -1, 1))]
        if step == 4:
            score(mine, (kv,))
            score((0, 1), blocks_of[0])
            up, (guests, held) = tie(up, (guests, held))
        if step == 5:
            score((2, 3), blocks_of[1])
            score((4, 5), blocks_of[2])
            up, held = tie(up, held)
        up = shifted(up, 1)
        down = shifted(down, -1)
        blocks_of.append((up, down))
    score((6, 7), blocks_of[3])
    score((8, 9), blocks_of[4])
    out = place_rows(where, held, held_spots, group_rows, None, packed.shape)
    up, out = tie(up, out)
    back = attend_guests([guests[2], *guests[:2]], (1, 0, 0), (up, down), group_rows)
    back = [shifted(g, by) for g, by in zip(back, (-1, 2, 1))]
    held, held_spots = [], []
    score((2 * far - 2, 2 * far - 1), (up, down))
    out = place_rows(
        where, [*held, *back], [*held_spots, ahead_far, opposite, behind_far], group_rows, out, packed.shape
    )
    return out[None, None]


def solution(mesh):
    return jax.shard_map(
        body,
        mesh=mesh,
        in_specs=(
            P("prompt", "dp", None, None),
            P("prompt", "dp", None),
            P("prompt", "dp", None),
            P("prompt", "dp", None),
            P("prompt", "dp", None),
            P("dp", "prompt", None, None),
        ),
        out_specs=P("prompt", "dp", None, None),
        check_vma=False,
    )
```
